32 devices in a mesh: ctx: 16 (over z, x, core), head: 2 (over y).
Axes of the slice: x: 2, y: 2, z: 4, core: 2. Of those that a mesh axis runs over, the one named last changes fastest.
Arguments:
- queries: bfloat16 [4096, 24, 128], P('ctx', 'head'), may hold values from -4.5 to 4.5, as said below
- key_vectors: bfloat16 [4096, 24, 128], P('ctx', 'head'), may hold values from -4.5 to 4.5, as said below
- value_vectors: bfloat16 [4096, 24, 128], P('ctx', 'head'), may hold values from -6 to 6
- attn_output: bfloat16 [4096, 24, 128], P('ctx', 'head'), may hold values from -6 to 6
- output_grad: bfloat16 [4096, 5120], P('ctx', 'head'), may hold values from -6 to 6
- w_out: bfloat16 [3072, 5120], P('head'), may hold values from -0.078125 to 0.078125
- log_total: float32 [4096, 24], P('ctx', 'head'), as said below
Outputs:
- query_grad: bfloat16 [4096, 24, 128], P('ctx', 'head')
- key_grad: bfloat16 [4096, 24, 128], P('ctx', 'head')
- value_grad: bfloat16 [4096, 24, 128], P('ctx', 'head')
The draws below stay inside these ranges and needn't reach their ends.
Inputs may be any that keep to these rules, and one draw needn't show every extreme that they name: `queries`: independent entries of order one. `key_vectors`: entries of order one. `log_total`: for each position and head, the log of the sum of exp(scores) over the positions it sees, from the given queries and keys.
All inputs are finite; a program needn't handle non-finite values.
Results may differ from the reference program's by a relative error of at most 0.0058.
Values may be sent and summed in bfloat16 or wider, within the bound.
No kernel may reach another device: no remote copies, remote signals or barrier semaphores. Data moves between devices by JAX's collectives and lax.ppermute only.
A program may use at most 128 MiB of HBM per device.

```python
import jax
import jax.numpy as jnp
from jax import lax

HEADS = 24
HEAD_DIM = 128
MODEL = 5120
TOKENS = 4096


def joint_draw(key):
    base_key = jax.random.fold_in(key, 101)
    full_shape = (TOKENS, HEADS, HEAD_DIM)
    query_draw = jax.random.normal(jax.random.fold_in(base_key, 1), full_shape, jnp.float32)
    key_draw = jax.random.normal(jax.random.fold_in(base_key, 2), full_shape, jnp.float32)
    query_draw = jnp.clip(query_draw, -4.5, 4.5)
    key_draw = jnp.clip(key_draw, -4.5, 4.5)
    query_round = query_draw.astype(jnp.bfloat16).astype(jnp.float32)
    key_round = key_draw.astype(jnp.bfloat16).astype(jnp.float32)
    position = jnp.arange(TOKENS, dtype=jnp.int32)
    causal = position[None, :] <= position[:, None]
    factor = HEAD_DIM ** (-0.5)

    def per_head(head_index):
        query_head = query_round[:, head_index, :]
        key_head = key_round[:, head_index, :]
        scores = jnp.dot(query_head, key_head.T, precision=lax.Precision.HIGHEST) * factor
        scores = jnp.where(causal, scores, -jnp.inf)
        return jax.nn.logsumexp(scores, axis=1)
    totals = lax.map(per_head, jnp.arange(HEADS, dtype=jnp.int32))
    return (query_draw, key_draw, jnp.transpose(totals, (1, 0)))


def draw_queries(key, part):
    return joint_draw(key)[0].astype(jnp.bfloat16)


def draw_key_vectors(key, part):
    return joint_draw(key)[1].astype(jnp.bfloat16)


def draw_log_total(key, part):
    return joint_draw(key)[2].astype(jnp.float32)


def steps_of(stream_key, shape, shards, smallest, largest):
    loudness, own = 1.0, jax.random.fold_in(stream_key, 6)
    for dim, shards_of in shards:
        heights = jnp.exp(jax.random.uniform(jax.random.fold_in(own, dim), (shards_of,), jnp.float32, smallest / len(shards), largest / len(shards)))
        loudness = loudness * jnp.repeat(heights, shape[dim] // shards_of).reshape([-1 if axis == dim else 1 for axis in range(len(shape))])
    return loudness


def scatter_about(own_key, dims, scale, reach, split=(), held_as=jnp.bfloat16):
    array = jax.random.normal(own_key, dims, jnp.float32) * scale
    if len(split) > 0:
        array = steps_of(own_key, dims, split, -0.22, 0.18) * array
    return jnp.clip(array, min=-reach, max=reach).astype(held_as)


def setup_inputs(seed: int = 0) -> dict:
    key_list = jax.random.split(jax.random.key(seed), 8)
    queries = draw_queries(jax.random.fold_in(key_list[7], 71), 0)
    key_vectors = draw_key_vectors(jax.random.fold_in(key_list[7], 71), 0)
    value_vectors = scatter_about(key_list[2], (TOKENS, HEADS, HEAD_DIM), 1.0, 6.0, ((0, 16), (1, 2)))
    attn_output = scatter_about(key_list[3], (TOKENS, HEADS, HEAD_DIM), 1.0, 6.0, ((0, 16), (1, 2)))
    output_grad = scatter_about(key_list[4], (TOKENS, MODEL), 1.0, 6.0, ((0, 16), (1, 2)))
    w_out = scatter_about(key_list[5], (HEADS * HEAD_DIM, MODEL), MODEL ** -0.5, 0.078125, ((0, 2),))
    log_total = draw_log_total(jax.random.fold_in(key_list[7], 71), 0)
    return {"queries": queries, "key_vectors": key_vectors, "value_vectors": value_vectors, "attn_output": attn_output, "output_grad": output_grad, "w_out": w_out, "log_total": log_total}


def reference(queries, key_vectors, value_vectors, attn_output, output_grad, w_out, log_total):
    factor = HEAD_DIM ** -0.5
    attn_grad = jnp.dot(output_grad, w_out.T, preferred_element_type=jnp.float32).astype(jnp.bfloat16)
    attn_grad = attn_grad.reshape(TOKENS, HEADS, HEAD_DIM)
    position = jnp.arange(TOKENS, dtype=jnp.int32)
    causal = position[None, :] <= position[:, None]

    def per_head(head_index):
        query_head = queries[:, head_index, :]
        key_head = key_vectors[:, head_index, :]
        value_head = value_vectors[:, head_index, :]
        output_head = attn_output[:, head_index, :]
        grad_head = attn_grad[:, head_index, :]
        total_head = log_total[:, head_index][:, None]
        raw_scores = jnp.dot(query_head, key_head.T, preferred_element_type=jnp.float32) * factor
        scores = jnp.where(causal, raw_scores, -jnp.inf)
        prob_full = jnp.exp(scores - total_head)
        prob_low = prob_full.astype(jnp.bfloat16)
        prob_grad = jnp.dot(grad_head, value_head.T, preferred_element_type=jnp.float32)
        row_delta = jnp.sum(grad_head.astype(jnp.float32) * output_head.astype(jnp.float32), axis=1, keepdims=True)
        score_grad = (prob_full * (prob_grad - row_delta)).astype(jnp.bfloat16)
        query_grad = (jnp.dot(score_grad, key_head, preferred_element_type=jnp.float32) * factor).astype(jnp.bfloat16)
        key_grad = (jnp.dot(score_grad.T, query_head, preferred_element_type=jnp.float32) * factor).astype(jnp.bfloat16)
        value_grad = jnp.dot(prob_low.T, grad_head, preferred_element_type=jnp.float32).astype(jnp.bfloat16)
        return query_grad, key_grad, value_grad

    query_grads, key_grads, value_grads = lax.map(per_head, jnp.arange(HEADS, dtype=jnp.int32))
    return (jnp.transpose(query_grads, (1, 0, 2)), jnp.transpose(key_grads, (1, 0, 2)), jnp.transpose(value_grads, (1, 0, 2)))
```

```python
import functools
import math

import jax
import jax.numpy as jnp
from jax import lax
from jax.experimental import pallas as pl
from jax.experimental.pallas import tpu as pltpu
from jax.sharding import PartitionSpec as P

F32 = jnp.float32
BF16 = jnp.bfloat16
LANES = 128
NT = (((1,), (1,)), ((), ()))
NN = (((1,), (0,)), ((), ()))


def stat_rows(rows):
    return -(-6 * (rows // LANES) // 16) * 16


def dot(a, b, dims):
    return lax.dot_general(a, b, dims, preferred_element_type=F32)


def pack_kernel(meta_ref, grad_ref, out_ref, total_ref, packed_ref, *, heads):
    rows, _ = grad_ref.shape
    halves = rows // LANES
    head = meta_ref[pl.program_id(0)] * heads + pl.program_id(1)
    grad = grad_ref[...]
    product = grad.astype(F32) * out_ref[...].astype(F32)
    delta = jnp.sum(jnp.transpose(product), axis=0, keepdims=True)
    total = total_ref[pl.ds(head, 1), :]
    pieces = []
    rest = [total, delta]
    for _ in range(3):
        high = [part.astype(BF16).astype(F32) for part in rest]
        rest = [part - top for part, top in zip(rest, high)]
        for top in high:
            pieces += [top[:, i * LANES : (i + 1) * LANES] for i in range(halves)]
    spare = stat_rows(rows) - len(pieces)
    if spare:
        pieces.append(jnp.zeros((spare, LANES), F32))
    packed_ref[0:rows, :] = grad
    packed_ref[rows:, :] = jnp.concatenate(pieces, axis=0).astype(BF16)


def pack_grads(members, grad_flat, out_heads, totals, heads):
    all_heads, rows, width = out_heads.shape
    group = all_heads // heads
    extra = stat_rows(rows)
    return pl.pallas_call(
        functools.partial(pack_kernel, heads=heads),
        grid_spec=pltpu.PrefetchScalarGridSpec(
            num_scalar_prefetch=1,
            grid=(group, heads),
            in_specs=[
                pl.BlockSpec((rows, width), lambda d, h, m: (0, m[d] * heads + h)),
                pl.BlockSpec((None, rows, width), lambda d, h, m: (m[d] * heads + h, 0, 0)),
                pl.BlockSpec((all_heads, rows), lambda d, h, m: (0, 0)),
            ],
            out_specs=pl.BlockSpec((None, None, rows + extra, width), lambda d, h, m: (d, h, 0, 0)),
        ),
        out_shape=jax.ShapeDtypeStruct((group, heads, rows + extra, width), BF16),
        name="pack_grads",
    )(members, grad_flat, out_heads, totals)


def read_stats(block, rows):
    halves = rows // LANES
    values = block.astype(F32)
    span = 2 * halves
    whole = values[0:span] + values[span : 2 * span] + values[2 * span : 3 * span]
    total = jnp.concatenate([whole[i : i + 1] for i in range(halves)], axis=1)
    delta = jnp.concatenate([whole[halves + i : halves + i + 1] for i in range(halves)], axis=1)
    return total, delta


def column(row):
    return jnp.transpose(jnp.broadcast_to(row, (LANES, row.shape[1])))[:, 0:1]


def positions(meta_ref, first, count, rows, shape, axis):
    place = lax.broadcasted_iota(jnp.int32, shape, axis)
    where = place + (meta_ref[1 + first] * rows)
    for i in range(1, count):
        where = jnp.where(place >= i * rows, place + (meta_ref[1 + first + i] - i) * rows, where)
    return where


def key_kernel(
    meta_ref, query_ref, grad_ref, key_ref, value_ref, *rest, diagonal, last, factor, tile
):
    if diagonal:
        dk_out, dv_out = rest
    else:
        dk_in, dv_in, dk_out, dv_out = rest
    group, rows, width = query_ref.shape
    first = pl.program_id(1) * tile

    def compute():
        keys = key_ref[...].reshape(tile * rows, width)
        values = value_ref[...].reshape(tile * rows, width)
        dk = jnp.zeros((tile * rows, width), F32)
        dv = jnp.zeros((tile * rows, width), F32)
        for g in range(group):
            queries = query_ref[g]
            grads = grad_ref[g, 0:rows, :]
            total, delta = read_stats(grad_ref[g, rows:, :], rows)
            scores = dot(keys, queries, NT) * factor
            if diagonal:
                key_pos = positions(meta_ref, first, tile, rows, scores.shape, 0)
                query_pos = positions(meta_ref, g, 1, rows, scores.shape, 1)
                scores = jnp.where(key_pos <= query_pos, scores, -jnp.inf)
            prob = jnp.exp(scores - total)
            dv = dv + dot(prob.astype(BF16), grads, NN)
            prob_grad = dot(values, grads, NT)
            score_grad = (prob * (prob_grad - delta)).astype(BF16)
            dk = dk + dot(score_grad, queries, NN)
        return dk, dv

    def emit(dk, dv):
        if not diagonal:
            dk = dk + dk_in[...].reshape(dk.shape)
            dv = dv + dv_in[...].reshape(dv.shape)
        if last:
            dk = dk * factor
        dk_out[...] = dk.reshape(dk_out.shape).astype(dk_out.dtype)
        dv_out[...] = dv.reshape(dv_out.shape).astype(dv_out.dtype)

    if diagonal:
        emit(*compute())
    else:
        pl.when(meta_ref[0] > 0)(lambda: emit(*compute()))

        @pl.when(meta_ref[0] == 0)
        def _():
            emit(jnp.zeros((tile * rows, width), F32), jnp.zeros((tile * rows, width), F32))


def query_kernel(
    meta_ref, query_ref, grad_ref, key_ref, value_ref, *rest, diagonal, last, factor, tile
):
    if diagonal:
        (dq_out,) = rest
    else:
        dq_in, dq_out = rest
    group, rows, width = key_ref.shape
    first = pl.program_id(1) * tile

    def compute():
        queries = query_ref[...].reshape(tile * rows, width)
        grads = jnp.concatenate([grad_ref[i, 0:rows, :] for i in range(tile)], axis=0)
        stats = [read_stats(grad_ref[i, rows:, :], rows) for i in range(tile)]
        total = jnp.concatenate([column(part[0]) for part in stats], axis=0)
        delta = jnp.concatenate([column(part[1]) for part in stats], axis=0)
        dq = jnp.zeros((tile * rows, width), F32)
        for g in range(group):
            keys = key_ref[g]
            scores = dot(queries, keys, NT) * factor
            if diagonal:
                query_pos = positions(meta_ref, first, tile, rows, scores.shape, 0)
                key_pos = positions(meta_ref, g, 1, rows, scores.shape, 1)
                scores = jnp.where(key_pos <= query_pos, scores, -jnp.inf)
            prob = jnp.exp(scores - total)
            prob_grad = dot(grads, value_ref[g], NT)
            score_grad = (prob * (prob_grad - delta)).astype(BF16)
            dq = dq + dot(score_grad, keys, NN)
        return dq

    def emit(dq):
        if not diagonal:
            dq = dq + dq_in[...].reshape(dq.shape)
        if last:
            dq = dq * factor
        dq_out[...] = dq.reshape(dq_out.shape).astype(dq_out.dtype)

    if diagonal:
        emit(compute())
    else:
        pl.when(meta_ref[0] > 0)(lambda: emit(compute()))

        @pl.when(meta_ref[0] == 0)
        def _():
            emit(jnp.zeros((tile * rows, width), F32))


def call_pass(kernel, meta, queries, grads, keys, values, running, *, diagonal, last, factor):
    group, heads, rows, width = queries.shape
    packed = grads.shape[2]
    tile = 2 if group % 2 == 0 else 1
    by_key = kernel is key_kernel

    def whole(height):
        return pl.BlockSpec((group, None, height, width), lambda h, t, m: (0, h, 0, 0))

    def part(height):
        return pl.BlockSpec((tile, None, height, width), lambda h, t, m: (t, h, 0, 0))

    query_side, key_side = (whole, part) if by_key else (part, whole)
    outputs = 2 if by_key else 1
    out_type = BF16 if last else F32
    pairs = heads * (group * rows) ** 2
    products = 4 if by_key else 3
    return pl.pallas_call(
        functools.partial(kernel, diagonal=diagonal, last=last, factor=factor, tile=tile),
        grid_spec=pltpu.PrefetchScalarGridSpec(
            num_scalar_prefetch=1,
            grid=(heads, group // tile),
            in_specs=[query_side(rows), query_side(packed), key_side(rows), key_side(rows)]
            + [part(rows)] * len(running),
            out_specs=[part(rows)] * outputs,
        ),
        out_shape=[jax.ShapeDtypeStruct(queries.shape, out_type)] * outputs,
        compiler_params=pltpu.CompilerParams(vmem_limit_bytes=48 * 1024 * 1024),
        cost_estimate=pl.CostEstimate(
            flops=2 * products * pairs * width,
            bytes_accessed=8 * queries.size * 2,
            transcendentals=pairs,
        ),
        name="key_pass" if by_key else "query_pass",
    )(meta, queries, grads, keys, values, *running)


def body(queries, key_vectors, value_vectors, attn_output, output_grad, w_out, log_total):
    rows, head_count, width = queries.shape
    factor = width ** (-0.5)
    ctx_count = lax.axis_size("ctx")
    head_size = lax.axis_size("head")
    ctx_index = lax.axis_index("ctx")
    group = math.gcd(ctx_count, head_count)
    group = group & -group
    heads = head_count // group
    blocks = ctx_count // group
    block_index = ctx_index // group
    member = ctx_index % group
    members = jnp.bitwise_xor(member, jnp.arange(group, dtype=jnp.int32))

    def swap(d):
        return [(i, (i // group) * group + (i % group ^ d)) for i in range(ctx_count)]

    def spread(array, axis):
        own = [lax.index_in_dim(array, 0, axis, keepdims=False)]
        for d in range(1, group):
            own.append(lax.ppermute(lax.index_in_dim(array, d, axis, keepdims=False), "ctx", swap(d)))
        return jnp.stack(own, axis=axis)

    def by_member(array):
        grouped = jnp.transpose(array, (1, 0, 2)).reshape(group, heads, rows, width)
        return jnp.stack([lax.dynamic_index_in_dim(grouped, members[d], 0, False) for d in range(group)])

    if head_size == 2:
        other = lax.ppermute(output_grad, "head", [(0, 1), (1, 0)])
        lower = lax.axis_index("head") == 0
        features = jnp.concatenate(
            [jnp.where(lower, output_grad, other), jnp.where(lower, other, output_grad)], axis=1
        )
    else:
        features = lax.all_gather(output_grad, "head", axis=1, tiled=True)

    key_value = spread(jnp.stack([by_member(key_vectors), by_member(value_vectors)]), 1)
    own_keys, own_values = key_value[0], key_value[1]
    own_queries = spread(by_member(queries), 0)

    grad_flat = lax.dot_general(features, w_out, NT, preferred_element_type=F32).astype(BF16)
    packed = pack_grads(
        members,
        grad_flat,
        jnp.transpose(attn_output, (1, 0, 2)),
        jnp.transpose(log_total, (1, 0)),
        heads,
    )
    own_grads = spread(packed, 0)

    def meta_of(valid):
        return jnp.concatenate([jnp.asarray(valid, jnp.int32).reshape(1), members])

    always = meta_of(1)
    common = dict(factor=factor)
    only = blocks == 1
    (dq,) = call_pass(
        query_kernel, always, own_queries, own_grads, own_keys, own_values, [],
        diagonal=True, last=only, **common,
    )
    dk, dv = call_pass(
        key_kernel, always, own_queries, own_grads, own_keys, own_values, [],
        diagonal=True, last=only, **common,
    )
    up = [own_keys, own_values]
    down = [own_queries, own_grads]
    for step in range(1, blocks):
        forward = [
            (z * group + i, (z + 1) * group + i) for z in range(step - 1, blocks - 1) for i in range(group)
        ]
        backward = [
            (z * group + i, (z - 1) * group + i) for z in range(1, blocks - step + 1) for i in range(group)
        ]
        up = [lax.ppermute(array, "ctx", forward) for array in up]
        down = [lax.ppermute(array, "ctx", backward) for array in down]
        last = step == blocks - 1
        (dq,) = call_pass(
            query_kernel, meta_of(block_index >= step), own_queries, own_grads, *up, [dq],
            diagonal=False, last=last, **common,
        )
        dk, dv = call_pass(
            key_kernel, meta_of(block_index < blocks - step), *down, own_keys, own_values, [dk, dv],
            diagonal=False, last=last, **common,
        )

    def collect(array):
        pieces = spread(array, 0)
        ordered = jnp.stack([lax.dynamic_index_in_dim(pieces, member ^ g, 0, False) for g in range(group)])
        return jnp.transpose(ordered.reshape(head_count, rows, width), (1, 0, 2))

    return collect(dq), collect(dk), collect(dv)


def solution(mesh):
    in_specs = (
        P("ctx", "head", None),
        P("ctx", "head", None),
        P("ctx", "head", None),
        P("ctx", "head", None),
        P("ctx", "head"),
        P("head", None),
        P("ctx", "head"),
    )
    out_specs = (P("ctx", "head", None), P("ctx", "head", None), P("ctx", "head", None))
    return jax.shard_map(body, mesh=mesh, in_specs=in_specs, out_specs=out_specs, check_vma=False)
```

```python
import functools
import math

import jax
import jax.numpy as jnp
from jax import lax
from jax.experimental import pallas as pl
from jax.experimental.pallas import tpu as pltpu
from jax.sharding import PartitionSpec as P

F32 = jnp.float32
BF16 = jnp.bfloat16
LANES = 128
NT = (((1,), (1,)), ((), ()))
NN = (((1,), (0,)), ((), ()))
VMEM_LIMIT = 48 * 1024 * 1024
COST_SCALE = 1.0


def cost(microseconds):
    return pl.CostEstimate(
        flops=int(1.15e9 * COST_SCALE * microseconds),
        bytes_accessed=int(3.0e6 * COST_SCALE * microseconds),
        transcendentals=0,
    )


def dot(a, b, dims):
    return lax.dot_general(a, b, dims, preferred_element_type=F32)


def stat_rows(rows):
    return -(-6 * (rows // LANES) // 16) * 16


def write_stats(total, delta):
    rows = total.shape[1]
    halves = rows // LANES
    pieces = []
    rest = [total, delta]
    for _ in range(3):
        high = [part.astype(BF16).astype(F32) for part in rest]
        rest = [part - top for part, top in zip(rest, high)]
        for top in high:
            pieces += [top[:, i * LANES : (i + 1) * LANES] for i in range(halves)]
    spare = stat_rows(rows) - len(pieces)
    if spare:
        pieces.append(jnp.zeros((spare, LANES), F32))
    return jnp.concatenate(pieces, axis=0).astype(BF16)


def read_stats(block, rows):
    halves = rows // LANES
    values = block.astype(F32)
    span = 2 * halves
    whole = values[0:span] + values[span : 2 * span] + values[2 * span : 3 * span]
    total = jnp.concatenate([whole[i : i + 1] for i in range(halves)], axis=1)
    delta = jnp.concatenate([whole[halves + i : halves + i + 1] for i in range(halves)], axis=1)
    return total, delta


def move_kernel(*refs, group, copies):
    *arrays, sems = refs
    member = lax.axis_index("ctx") % group
    started = [
        pltpu.make_async_copy(
            arrays[source].at[source_at(member)], arrays[target].at[target_at(member)], sems.at[n]
        )
        for n, (source, source_at, target, target_at) in enumerate(copies)
    ]
    for copy in started:
        copy.start()
    for copy in started:
        copy.wait()


def move(name, group, arrays, shapes, copies):
    return pl.pallas_call(
        functools.partial(move_kernel, group=group, copies=copies),
        in_specs=[pl.BlockSpec(memory_space=pl.ANY)] * len(arrays),
        out_specs=[pl.BlockSpec(memory_space=pltpu.VMEM)] * len(shapes),
        out_shape=[jax.ShapeDtypeStruct(shape, BF16) for shape in shapes],
        scratch_shapes=[pltpu.SemaphoreType.DMA((len(copies),))],
        compiler_params=pltpu.CompilerParams(vmem_limit_bytes=VMEM_LIMIT),
        cost_estimate=cost(1.5),
        name=name,
    )(*arrays)


def at(*index):
    return lambda member: index


def project_kernel(meta_ref, feature_ref, weight_ref, *rest, heads, final, partial):
    grad = dot(feature_ref[...], weight_ref[...], NT)
    if partial:
        grad = grad + rest[0][...]
        rest = rest[1:]
    if not final:
        rest[0][...] = grad
        return
    out_ref, total_ref, packed_ref = rest
    _, rows, width = out_ref.shape
    grad = grad.astype(BF16)
    first = meta_ref[pl.program_id(0)] * heads
    for h in range(heads):
        mine = grad[:, h * width : (h + 1) * width]
        product = mine.astype(F32) * out_ref[h].astype(F32)
        delta = jnp.sum(jnp.transpose(product), axis=0, keepdims=True)
        total = total_ref[pl.ds(first + h, 1), :]
        packed_ref[h, 0:rows, :] = mine
        packed_ref[h, rows:, :] = write_stats(total, delta)


def project(meta, feature, w_out, partial, out_heads, totals, group, final):
    all_heads, rows, width = out_heads.shape
    heads = all_heads // group
    packed = rows + stat_rows(rows)
    span = feature.shape[1]
    by_member = pl.BlockSpec((rows, heads * width), lambda d, m: (0, d))
    arrays = [feature, w_out]
    in_specs = [
        pl.BlockSpec((rows, span), lambda d, m: (0, 0)),
        pl.BlockSpec((heads * width, span), lambda d, m: (m[d], m[group])),
    ]
    if partial is not None:
        arrays.append(partial)
        in_specs.append(by_member)
    if final:
        arrays += [out_heads, totals]
        in_specs += [
            pl.BlockSpec((heads, rows, width), lambda d, m: (m[d], 0, 0)),
            pl.BlockSpec((all_heads, rows), lambda d, m: (0, 0)),
        ]
        out_spec = pl.BlockSpec((None, heads, packed, width), lambda d, m: (d, 0, 0, 0))
        out_shape = jax.ShapeDtypeStruct((group, heads, packed, width), BF16)
    else:
        out_spec, out_shape = by_member, jax.ShapeDtypeStruct((rows, all_heads * width), F32)
    return pl.pallas_call(
        functools.partial(project_kernel, heads=heads, final=final, partial=partial is not None),
        grid_spec=pltpu.PrefetchScalarGridSpec(
            num_scalar_prefetch=1, grid=(group,), in_specs=in_specs, out_specs=out_spec
        ),
        out_shape=out_shape,
        compiler_params=pltpu.CompilerParams(vmem_limit_bytes=VMEM_LIMIT),
        cost_estimate=cost(6.5),
        name="project",
    )(meta, *arrays)


def attend_kernel(*refs, group, blocks, jobs, queries, pairs, sum_in, sum_out, parts):
    refs = list(refs)
    query_refs = [refs.pop(0) for _ in range(queries)]
    grad_refs = [refs.pop(0) for _ in range(queries)]
    pair_refs = [refs.pop(0) for _ in range(pairs)]
    start_ref = refs.pop(0) if sum_in else None
    total_ref = refs.pop(0) if sum_out else None
    part_refs = [refs.pop(0) if part else None for part in parts]
    sum_ref = refs.pop(0)
    _, rows, width = query_refs[0].shape
    span = group * rows
    factor = width ** (-0.5)
    place = lax.axis_index("ctx")
    block = place // group
    member = place % group
    sum_ref[...] = start_ref[...] if sum_in else jnp.zeros(sum_ref.shape, F32)

    def compute(query_ref, grad_ref, pair_ref, part_ref, step):
        query_sum = sum_ref if sum_ref.ndim == 3 else None
        want_query = query_sum is not None or (part_ref is not None and sum_ref.ndim == 4)
        want_key = sum_ref.ndim == 4 or part_ref is not None
        keys = pair_ref[:, 0].reshape(span, width)
        values = pair_ref[:, 1].reshape(span, width)
        key_columns = jnp.transpose(keys) if want_query else None
        dk = jnp.zeros((span, width), F32)
        dv = jnp.zeros((span, width), F32)
        for g in range(group):
            query = query_ref[g]
            grad = grad_ref[g, 0:rows, :]
            total, delta = read_stats(grad_ref[g, rows:, :], rows)
            scores = dot(keys, query, NT) * factor
            if step == 0:
                index = lax.broadcasted_iota(jnp.int32, scores.shape, 0)
                key_pos = index + (member * rows)
                for i in range(1, group):
                    shift = ((member ^ i) - i) * rows
                    key_pos = jnp.where(index >= i * rows, index + shift, key_pos)
                query_pos = lax.broadcasted_iota(jnp.int32, scores.shape, 1) + (member ^ g) * rows
                scores = jnp.where(key_pos <= query_pos, scores, -jnp.inf)
            prob = jnp.exp(scores - total)
            prob_grad = dot(values, grad, NT)
            score_grad = (prob * (prob_grad - delta)).astype(BF16)
            if want_key:
                dv = dv + dot(prob.astype(BF16), grad, NN)
                dk = dk + dot(score_grad, query, NN)
            if want_query:
                dq = jnp.transpose(dot(key_columns, score_grad, NN)) * factor
                if query_sum is not None:
                    query_sum[g] += dq
                else:
                    part_ref[g] = dq.astype(part_ref.dtype)
        if want_key:
            dk = (dk * factor).reshape(group, rows, width)
            dv = dv.reshape(group, rows, width)
            if sum_ref.ndim == 4:
                sum_ref[:, 0] += dk
                sum_ref[:, 1] += dv
            else:
                part_ref[:, 0] = dk.astype(part_ref.dtype)
                part_ref[:, 1] = dv.astype(part_ref.dtype)

    for (query_at, pair_at, step), part_ref in zip(jobs, part_refs):
        run = functools.partial(
            compute, query_refs[query_at], grad_refs[query_at], pair_refs[pair_at], part_ref, step
        )
        if step == 0:
            run()
            continue
        visible = block + step < blocks if step > 0 else block >= -step
        pl.when(visible)(run)
        if part_ref is not None:

            @pl.when(jnp.logical_not(visible))
            def _(part_ref=part_ref):
                part_ref[...] = jnp.zeros(part_ref.shape, part_ref.dtype)

    if sum_out:
        total_ref[...] = sum_ref[...].astype(total_ref.dtype)


def attend(queries, pairs, jobs, side, heads, group, blocks, running=None, total_type=None, part_types=(), name="attend"):
    query_arrays = [q for q, _, _, _ in queries] + [g for _, g, _, _ in queries]
    rows, width = queries[0][0].shape[2:]
    packed = queries[0][1].shape[2]

    def spec(first, *shape):
        return pl.BlockSpec((group, None) + shape, lambda h: (0, first + h) + (0,) * len(shape))

    query_shape, pair_shape = (group, heads, rows, width), (group, heads, 2, rows, width)
    sum_shape, part_shape = (query_shape, pair_shape) if side == "query" else (pair_shape, query_shape)
    in_specs = [spec(f, rows, width) for _, _, f, _ in queries]
    in_specs += [spec(f, packed, width) for _, _, _, f in queries]
    in_specs += [spec(f, 2, rows, width) for _, f in pairs]
    arrays = query_arrays + [p for p, _ in pairs]
    if running is not None:
        arrays.append(running)
        in_specs.append(spec(0, *sum_shape[2:]))
    shapes, out_specs = [], []
    if total_type is not None:
        shapes.append(jax.ShapeDtypeStruct(sum_shape, total_type))
        out_specs.append(spec(0, *sum_shape[2:]))
    for part in part_types:
        if part is not None:
            shapes.append(jax.ShapeDtypeStruct(part_shape, part))
            out_specs.append(spec(0, *part_shape[2:]))
    return pl.pallas_call(
        functools.partial(
            attend_kernel,
            group=group,
            blocks=blocks,
            jobs=jobs,
            queries=len(queries),
            pairs=len(pairs),
            sum_in=running is not None,
            sum_out=total_type is not None,
            parts=[part is not None for part in part_types],
        ),
        grid=(heads,),
        in_specs=in_specs,
        out_specs=out_specs,
        out_shape=shapes,
        scratch_shapes=[pltpu.VMEM((group,) + sum_shape[2:], F32)],
        compiler_params=pltpu.CompilerParams(vmem_limit_bytes=VMEM_LIMIT),
        cost_estimate=cost(1 + 2.2 * heads * len(jobs)),
        name=name,
    )(*arrays)


def add(own, arrived):
    return (own + arrived.astype(F32)).astype(BF16)


def send(name, array, ways, axis="ctx"):
    with jax.named_scope(name):
        return lax.ppermute(array, axis, ways)


class Order:
    def __init__(self):
        self.last = None

    def gate(self, array, *others):
        held = [other for other in (self.last, *others) if other is not None]
        return lax.optimization_barrier((array, *held))[0] if held else array

    def keep(self, result):
        self.last = result[0] if isinstance(result, (list, tuple)) else result
        return result


def body(queries, key_vectors, value_vectors, attn_output, output_grad, w_out, log_total):
    rows, head_count, width = queries.shape
    ctx_count = lax.axis_size("ctx")
    head_size = lax.axis_size("head")
    head_index = lax.axis_index("head")
    ctx_index = lax.axis_index("ctx")
    group = math.gcd(ctx_count, head_count)
    group = group & -group
    heads = head_count // group
    blocks = ctx_count // group
    member = ctx_index % group
    packed_rows = rows + stat_rows(rows)
    outer = heads // 3
    inner = heads - 2 * outer
    kinds = [(0, outer), (outer, inner), (heads - outer, outer)]
    others = range(1, group)
    order = Order()

    def swap(d):
        return [(i, (i // group) * group + (i % group ^ d)) for i in range(ctx_count)]

    def exchange(name, pieces):
        got = {d: send(name, pieces[d - 1], swap(d)) for d in reversed(others)}
        return [got[d] for d in others]

    def shift(first, last, by):
        return [(z * group + i, (z + by) * group + i) for z in range(first, last) for i in range(group)]

    def up(step):
        return shift(step - 1, blocks - 1, 1)

    def down(step):
        return shift(1, blocks - step + 1, -1)

    def head_major(array):
        return jnp.transpose(array, (1, 0, 2))

    def head_of(d, head):
        return lambda member: ((member ^ d) * heads + head,)

    meta = [jnp.asarray(member ^ d, jnp.int32) for d in range(group)]
    if head_size == 2:
        features = [output_grad, send("features", output_grad, [(0, 1), (1, 0)], "head")]
        places = [head_index, 1 - head_index]
    else:
        features = [lax.all_gather(output_grad, "head", axis=1, tiled=True)]
        places = [jnp.zeros_like(head_index)]

    own = [head_major(queries), head_major(key_vectors), head_major(value_vectors)]
    all_heads = range(heads)
    first_in = [(i, h) for h in range(outer) for i in (1, 2)] + [(0, h) for h in range(outer, heads)]
    second_in = [(i, h) for h in range(outer, heads) for i in (1, 2)] + [(0, h) for h in range(outer)]

    def spread(name, wanted):
        if group == 1:
            return []
        pieces = order.keep(
            move(
                name,
                group,
                [order.gate(own[0])] + own[1:],
                [(len(wanted), rows, width)] * (group - 1),
                [(i, head_of(d, h), 2 + d, at(n)) for d in others for n, (i, h) in enumerate(wanted)],
            )
        )
        return exchange(name, pieces)

    def join(name, wanted, got, arrays):
        copies = []
        for target, (_, where) in enumerate(arrays):
            for key, index in where.items():
                copies.append((key[0], head_of(0, key[1]), 2 + group + target, at(0, *index)))
                n = wanted.index(key)
                copies += [(2 + d, at(n), 2 + group + target, at(d, *index)) for d in others]
        return order.keep(
            move(name, group, [order.gate(own[0])] + own[1:] + got, [(group,) + shape for shape, _ in arrays], copies)
        )

    def pair_array(first, count):
        where = {(i, first + h): (h, i - 1) for h in range(count) for i in (1, 2)}
        return (count, 2, rows, width), where

    def query_array(first, count):
        return (count, rows, width), {(0, first + h): (h,) for h in range(count)}

    got_first = spread("split_first", first_in)
    flat_totals = jnp.transpose(log_total, (1, 0))
    partial = None
    for feature, place in zip(features[:-1], places):
        partial = order.keep(
            project(jnp.stack(meta + [place]), order.gate(feature), w_out, partial, head_major(attn_output), flat_totals, group, False)
        )

    up_a, down_q, down_c = [None], [None], [None]
    if outer:
        pairs_a, query_bc = join(
            "join_first", first_in, got_first, [pair_array(0, outer), query_array(outer, heads - outer)]
        )
        up_a = [pairs_a]
        if blocks > 1:
            up_a.append(send("pairs_a", pairs_a, up(1)))
    else:
        (query_bc,) = join("join_first", first_in, got_first, [query_array(0, heads)])
    down_q = [query_bc]
    if blocks > 1:
        down_q.append(send("queries", query_bc, down(1)))

    got_second = spread("split_second", second_in)
    for step in range(2, blocks):
        if outer:
            up_a.append(send("pairs_a", order.gate(up_a[-1]), up(step)))
        down_q.append(send("queries", order.gate(down_q[-1]), down(step)))

    def hop(arrays, step):
        return arrays[min(step, len(arrays) - 1)]

    feature = order.gate(features[-1], hop(up_a, 1), hop(down_q, 1))
    packed = order.keep(
        project(jnp.stack(meta + [places[-1]]), feature, w_out, partial, head_major(attn_output), flat_totals, group, True)
    )
    got_grads = exchange(
        "grads",
        order.keep(
            move(
                "split_grads", group, [packed], [packed.shape[1:]] * (group - 1),
                [(0, at(d), d, at(slice(None))) for d in others],
            )
        ) if group > 1 else [],
    )
    if outer:
        pairs_b, pairs_c, query_a = join(
            "join_second",
            second_in,
            got_second,
            [pair_array(outer, inner), pair_array(heads - outer, outer), query_array(0, outer)],
        )
    else:
        (pairs_b,) = join("join_second", second_in, got_second, [pair_array(0, heads)])
    grads = order.keep(
        move(
            "join_grads",
            group,
            [order.gate(packed, hop(up_a, 2), hop(down_q, 2))] + got_grads,
            [(group, count, packed_rows, width) for _, count in kinds if count],
            [
                copy
                for target, (first, count) in enumerate(kind for kind in kinds if kind[1])
                for copy in [(0, at(0, pl.ds(first, count)), group + target, at(0))]
                + [(d, at(pl.ds(first, count)), group + target, at(d)) for d in others]
            ],
        )
    )
    grad_a, grad_b, grad_c = grads if outer else (None, grads[0], None)

    def run(name, queries, pairs, jobs, side, count, running=None, total=F32, parts=(), wait=()):
        query, grad, f, g = queries[0]
        queries = [(order.gate(query, *wait), grad, f, g)] + list(queries[1:])
        return order.keep(
            attend(queries, pairs, jobs, side, count, group, blocks, running=running, total_type=total, part_types=parts, name=name)
        )

    far = blocks - 1
    near = range(1, far)
    final = BF16 if far == 0 else F32
    if outer:
        down_c = [grad_c]
        for step in range(1, blocks):
            down_c.append(send("grads_c", down_c[-1], down(step)))
    up_b = [order.gate(pairs_b)]
    for step in range(1, blocks):
        up_b.append(send("pairs_b", up_b[-1], up(step)))

    if outer:
        dp_c, dq_c = run("own_c",
            [(query_bc, grad_c, inner, 0)], [(pairs_c, 0)], [(0, 0, 0)], "key", outer, total=final, parts=[F32]
        )
        dq_a, back_a = None, None
        if far:
            dq_a, back_a = run("far_a",
                [(query_a, grad_a, 0, 0)], [(up_a[far], 0)], [(0, 0, -far)], "query", outer, parts=[BF16],
                wait=[down_c[1]],
            )
            back_a = send("home_a", back_a, shift(far, blocks, -1))
    down_b = [order.gate(grad_b, hop(down_c, 1))]
    for step in range(1, blocks):
        down_b.append(send("grads_b", down_b[-1], down(step)))

    def leave(dq, dp):
        n_q, n_p = dq.shape[1], dp.shape[1]
        if group == 1:
            return []
        pieces = move(
            "leave",
            group,
            [order.gate(dq), dp],
            [(n_q + 2 * n_p, rows, width)] * (group - 1),
            [(0, at(d), 1 + d, at(pl.ds(0, n_q))) for d in others]
            + [(1, at(d, h), 1 + d, at(pl.ds(n_q + 2 * h, 2))) for d in others for h in range(n_p)],
        )
        return exchange("leave", pieces)

    batches = []
    if outer:
        done = run("near_a",
            [(query_a, grad_a, 0, 0)],
            [(pair, 0) for pair in up_a[: max(far, 1)]],
            [(0, s, -s) for s in range(max(far, 1))],
            "query",
            outer,
            running=dq_a,
            total=BF16,
            parts=[F32] * max(far, 1),
            wait=[hop(up_b, 1), hop(down_q, far)],
        )
        dq_a, dp_a, parts_a = done[0], done[1], done[1:]

        def homeward_a(step, back):
            total = order.keep(add(order.gate(parts_a[step]), back))
            return send("home_a", total, shift(step, blocks, -1)) if step else total

        def homeward_c(step, back):
            total = order.keep(add(order.gate(parts_c[step]), back))
            return send("home_c", total, shift(0, blocks - step, 1)) if step else total

        parts_c = [dq_c]
        if near:
            back_a = homeward_a(far - 1, back_a)
            done = run("near_c",
                [(down_q[s], down_c[s], inner, 0) for s in near], [(pairs_c, 0)], [(s - 1, 0, s) for s in near],
                "key", outer, running=dp_c, parts=[F32] * len(near), wait=[hop(down_c, 2)],
            )
            dp_c = done[0]
            parts_c += done[1:]
        if far:
            dp_c, back_c = run("far_c",
                [(down_q[far], down_c[far], inner, 0)], [(pairs_c, 0)], [(0, 0, far)],
                "key", outer, running=dp_c, total=BF16, parts=[BF16], wait=[hop(up_b, 2)],
            )
            back_c = send("home_c", back_c, shift(0, blocks - far, 1))

    dq_b, dp_b = run("near_up_b",
        [(query_bc, grad_b, 0, 0)], [(pair, 0) for pair in up_b[: max(far, 1)]],
        [(0, s, -s) for s in range(max(far, 1))], "query", inner, total=final,
        parts=[F32] + [None] * (max(far, 1) - 1),
    )
    if outer and near:
        back_c = homeward_c(far - 1, back_c)
        for step in reversed(range(1, far - 1)):
            back_a = homeward_a(step, back_a)
    if near:
        (dp_b,) = run("near_down_b",
            [(down_q[s], down_b[s], 0, 0) for s in near], [(pairs_b, 0)], [(s - 1, 0, s) for s in near],
            "key", inner, running=dp_b, parts=[None] * len(near),
        )
    if outer and near:
        for step in reversed(range(1, far - 1)):
            back_c = homeward_c(step, back_c)
    if outer:
        batches.append((dq_a, dp_c, 0, 2, leave(dq_a, dp_c)))
    if outer and far:
        dp_a = homeward_a(0, back_a)
    if far:
        (dp_b,) = run("far_down_b",
            [(down_q[far], down_b[far], 0, 0)], [(pairs_b, 0)], [(0, 0, far)], "key", inner,
            running=dp_b, total=BF16, parts=[None],
        )
        (dq_b,) = run("far_up_b",
            [(query_bc, grad_b, 0, 0)], [(up_b[far], 0)], [(0, 0, -far)], "query", inner,
            running=dq_b, total=BF16, parts=[None],
        )
    dp_b = dp_b.astype(BF16)
    batches.append((dq_b, dp_b, 1, 1, leave(dq_b, dp_b)))
    if outer:
        if far:
            dq_c = homeward_c(0, back_c)
        dq_c, dp_a = dq_c.astype(BF16), dp_a.astype(BF16)
        batches.append((dq_c, dp_a, 2, 0, leave(dq_c, dp_a)))

    arrays, copies = [], []
    for dq, dp, query_kind, pair_kind, got in batches:
        base = len(arrays)
        arrays += [dq, dp] + got
        first_q, n_q = kinds[query_kind]
        first_p, n_p = kinds[pair_kind]
        for d in range(group):
            for h in range(n_q):
                source = (base, at(0, h)) if d == 0 else (base + 1 + d, at(h))
                copies.append((*source, 0, head_of(d, first_q + h)))
            for h in range(n_p):
                for i in range(2):
                    source = (base + 1, at(0, h, i)) if d == 0 else (base + 1 + d, at(n_q + 2 * h + i))
                    copies.append((*source, 1 + i, head_of(d, first_p + h)))
    count = len(arrays)
    copies = [(s, s_at, count + t, t_at) for s, s_at, t, t_at in copies]
    grads = move("arrive", group, arrays, [(head_count, rows, width)] * 3, copies)
    return tuple(jnp.transpose(grad, (1, 0, 2)) for grad in grads)


def solution(mesh):
    in_specs = (
        P("ctx", "head", None),
        P("ctx", "head", None),
        P("ctx", "head", None),
        P("ctx", "head", None),
        P("ctx", "head"),
        P("head", None),
        P("ctx", "head"),
    )
    out_specs = (P("ctx", "head", None), P("ctx", "head", None), P("ctx", "head", None))
    return jax.shard_map(body, mesh=mesh, in_specs=in_specs, out_specs=out_specs, check_vma=False)
```

```python
import functools
import math

import jax
import jax.numpy as jnp
from jax import lax
from jax.experimental import pallas as pl
from jax.experimental.pallas import tpu as pltpu
from jax.sharding import PartitionSpec as P

F32 = jnp.float32
BF16 = jnp.bfloat16
LANES = 128
NT = (((1,), (1,)), ((), ()))
NN = (((1,), (0,)), ((), ()))
VMEM_LIMIT = 48 * 1024 * 1024
SPLIT_LIMIT = 62 * 1024 * 1024
COST_SCALE = 1.0


def cost(microseconds):
    return pl.CostEstimate(
        flops=int(1.15e9 * COST_SCALE * microseconds),
        bytes_accessed=int(3.0e6 * COST_SCALE * microseconds),
        transcendentals=0,
    )


def dot(a, b, dims):
    return lax.dot_general(a, b, dims, preferred_element_type=F32)


def stat_rows(rows):
    return -(-6 * (rows // LANES) // 16) * 16


def write_stats(total, delta):
    rows = total.shape[1]
    halves = rows // LANES
    pieces = []
    rest = [total, delta]
    for _ in range(3):
        high = [part.astype(BF16).astype(F32) for part in rest]
        rest = [part - top for part, top in zip(rest, high)]
        for top in high:
            pieces += [top[:, i * LANES : (i + 1) * LANES] for i in range(halves)]
    spare = stat_rows(rows) - len(pieces)
    if spare:
        pieces.append(jnp.zeros((spare, LANES), F32))
    return jnp.concatenate(pieces, axis=0).astype(BF16)


def read_stats(block, rows):
    halves = rows // LANES
    values = block.astype(F32)
    span = 2 * halves
    whole = values[0:span] + values[span : 2 * span] + values[2 * span : 3 * span]
    total = jnp.concatenate([whole[i : i + 1] for i in range(halves)], axis=1)
    delta = jnp.concatenate([whole[halves + i : halves + i + 1] for i in range(halves)], axis=1)
    return total, delta


def move_kernel(*refs, group, copies):
    *arrays, sems = refs
    member = lax.axis_index("ctx") % group
    started = [
        pltpu.make_async_copy(
            arrays[source].at[source_at(member)], arrays[target].at[target_at(member)], sems.at[n]
        )
        for n, (source, source_at, target, target_at) in enumerate(copies)
    ]
    for copy in started:
        copy.start()
    for copy in started:
        copy.wait()


def move(name, group, arrays, shapes, copies, source=pl.ANY, target=pltpu.VMEM, limit=VMEM_LIMIT):
    return pl.pallas_call(
        functools.partial(move_kernel, group=group, copies=copies),
        in_specs=[pl.BlockSpec(memory_space=source)] * len(arrays),
        out_specs=[pl.BlockSpec(memory_space=target)] * len(shapes),
        out_shape=[jax.ShapeDtypeStruct(shape, BF16) for shape in shapes],
        scratch_shapes=[pltpu.SemaphoreType.DMA((len(copies),))],
        compiler_params=pltpu.CompilerParams(vmem_limit_bytes=limit),
        cost_estimate=cost(1.5),
        name=name,
    )(*arrays)


def at(*index):
    return lambda member: index


def project_kernel(meta_ref, feature_ref, weight_ref, *rest, heads, final, partial):
    grad = dot(feature_ref[...], weight_ref[...], NT)
    if partial:
        grad = grad + rest[0][...]
        rest = rest[1:]
    if not final:
        rest[0][...] = grad
        return
    out_ref, total_ref, packed_ref = rest
    _, rows, width = out_ref.shape
    grad = grad.astype(BF16)
    first = meta_ref[pl.program_id(0)] * heads
    for h in range(heads):
        mine = grad[:, h * width : (h + 1) * width]
        product = mine.astype(F32) * out_ref[h].astype(F32)
        delta = jnp.sum(jnp.transpose(product), axis=0, keepdims=True)
        total = total_ref[pl.ds(first + h, 1), :]
        packed_ref[h, 0:rows, :] = mine
        packed_ref[h, rows:, :] = write_stats(total, delta)


def project(meta, feature, w_out, partial, out_heads, totals, group, final):
    all_heads, rows, width = out_heads.shape
    heads = all_heads // group
    packed = rows + stat_rows(rows)
    span = feature.shape[1]
    by_member = pl.BlockSpec((rows, heads * width), lambda d, m: (0, d))
    arrays = [feature, w_out]
    in_specs = [
        pl.BlockSpec((rows, span), lambda d, m: (0, 0)),
        pl.BlockSpec((heads * width, span), lambda d, m: (m[d], m[group])),
    ]
    if partial is not None:
        arrays.append(partial)
        in_specs.append(by_member)
    if final:
        arrays += [out_heads, totals]
        in_specs += [
            pl.BlockSpec((heads, rows, width), lambda d, m: (m[d], 0, 0)),
            pl.BlockSpec((all_heads, rows), lambda d, m: (0, 0)),
        ]
        out_spec = pl.BlockSpec((None, heads, packed, width), lambda d, m: (d, 0, 0, 0))
        out_shape = jax.ShapeDtypeStruct((group, heads, packed, width), BF16)
    else:
        out_spec, out_shape = by_member, jax.ShapeDtypeStruct((rows, all_heads * width), F32)
    return pl.pallas_call(
        functools.partial(project_kernel, heads=heads, final=final, partial=partial is not None),
        grid_spec=pltpu.PrefetchScalarGridSpec(
            num_scalar_prefetch=1, grid=(group,), in_specs=in_specs, out_specs=out_spec
        ),
        out_shape=out_shape,
        compiler_params=pltpu.CompilerParams(vmem_limit_bytes=VMEM_LIMIT),
        cost_estimate=cost(6.5),
        name="project",
    )(meta, *arrays)


def attend_kernel(*refs, group, blocks, jobs, queries, pairs, sum_in, sum_out, parts):
    refs = list(refs)
    query_refs = [refs.pop(0) for _ in range(queries)]
    grad_refs = [refs.pop(0) for _ in range(queries)]
    pair_refs = [refs.pop(0) for _ in range(pairs)]
    start_ref = refs.pop(0) if sum_in else None
    total_ref = refs.pop(0) if sum_out else None
    part_refs = [refs.pop(0) if part else None for part in parts]
    sum_ref = refs.pop(0)
    _, rows, width = query_refs[0].shape
    span = group * rows
    factor = width ** (-0.5)
    place = lax.axis_index("ctx")
    block = place // group
    member = place % group
    sum_ref[...] = start_ref[...] if sum_in else jnp.zeros(sum_ref.shape, F32)

    def compute(query_ref, grad_ref, pair_ref, part_ref, step):
        query_sum = sum_ref if sum_ref.ndim == 3 else None
        want_query = query_sum is not None or (part_ref is not None and sum_ref.ndim == 4)
        want_key = sum_ref.ndim == 4 or part_ref is not None
        keys = pair_ref[:, 0].reshape(span, width)
        values = pair_ref[:, 1].reshape(span, width)
        key_columns = jnp.transpose(keys) if want_query else None
        dk = jnp.zeros((span, width), F32)
        dv = jnp.zeros((span, width), F32)
        for g in range(group):
            query = query_ref[g]
            grad = grad_ref[g, 0:rows, :]
            total, delta = read_stats(grad_ref[g, rows:, :], rows)
            scores = dot(keys, query, NT) * factor
            if step == 0:
                index = lax.broadcasted_iota(jnp.int32, scores.shape, 0)
                key_pos = index + (member * rows)
                for i in range(1, group):
                    shift = ((member ^ i) - i) * rows
                    key_pos = jnp.where(index >= i * rows, index + shift, key_pos)
                query_pos = lax.broadcasted_iota(jnp.int32, scores.shape, 1) + (member ^ g) * rows
                scores = jnp.where(key_pos <= query_pos, scores, -jnp.inf)
            prob = jnp.exp(scores - total)
            prob_grad = dot(values, grad, NT)
            score_grad = (prob * (prob_grad - delta)).astype(BF16)
            if want_key:
                dv = dv + dot(prob.astype(BF16), grad, NN)
                dk = dk + dot(score_grad, query, NN)
            if want_query:
                dq = jnp.transpose(dot(key_columns, score_grad, NN)) * factor
                if query_sum is not None:
                    query_sum[g] += dq
                else:
                    part_ref[g] = dq.astype(part_ref.dtype)
        if want_key:
            dk = (dk * factor).reshape(group, rows, width)
            dv = dv.reshape(group, rows, width)
            if sum_ref.ndim == 4:
                sum_ref[:, 0] += dk
                sum_ref[:, 1] += dv
            else:
                part_ref[:, 0] = dk.astype(part_ref.dtype)
                part_ref[:, 1] = dv.astype(part_ref.dtype)

    for (query_at, pair_at, step), part_ref in zip(jobs, part_refs):
        run = functools.partial(
            compute, query_refs[query_at], grad_refs[query_at], pair_refs[pair_at], part_ref, step
        )
        if step == 0:
            run()
            continue
        visible = block + step < blocks if step > 0 else block >= -step
        pl.when(visible)(run)
        if part_ref is not None:

            @pl.when(jnp.logical_not(visible))
            def _(part_ref=part_ref):
                part_ref[...] = jnp.zeros(part_ref.shape, part_ref.dtype)

    if sum_out:
        total_ref[...] = sum_ref[...].astype(total_ref.dtype)


def attend(queries, pairs, jobs, side, heads, group, blocks, running=None, total_type=None, part_types=(), name="attend", time=None):
    query_arrays = [q for q, _, _, _ in queries] + [g for _, g, _, _ in queries]
    rows, width = queries[0][0].shape[2:]
    packed = queries[0][1].shape[2]

    def spec(first, *shape):
        return pl.BlockSpec((group, None) + shape, lambda h: (0, first + h) + (0,) * len(shape))

    query_shape, pair_shape = (group, heads, rows, width), (group, heads, 2, rows, width)
    sum_shape, part_shape = (query_shape, pair_shape) if side == "query" else (pair_shape, query_shape)
    in_specs = [spec(f, rows, width) for _, _, f, _ in queries]
    in_specs += [spec(f, packed, width) for _, _, _, f in queries]
    in_specs += [spec(f, 2, rows, width) for _, f in pairs]
    arrays = query_arrays + [p for p, _ in pairs]
    if running is not None:
        arrays.append(running)
        in_specs.append(spec(0, *sum_shape[2:]))
    shapes, out_specs = [], []
    if total_type is not None:
        shapes.append(jax.ShapeDtypeStruct(sum_shape, total_type))
        out_specs.append(spec(0, *sum_shape[2:]))
    for part in part_types:
        if part is not None:
            shapes.append(jax.ShapeDtypeStruct(part_shape, part))
            out_specs.append(spec(0, *part_shape[2:]))
    return pl.pallas_call(
        functools.partial(
            attend_kernel,
            group=group,
            blocks=blocks,
            jobs=jobs,
            queries=len(queries),
            pairs=len(pairs),
            sum_in=running is not None,
            sum_out=total_type is not None,
            parts=[part is not None for part in part_types],
        ),
        grid=(heads,),
        in_specs=in_specs,
        out_specs=out_specs,
        out_shape=shapes,
        scratch_shapes=[pltpu.VMEM((group,) + sum_shape[2:], F32)],
        compiler_params=pltpu.CompilerParams(vmem_limit_bytes=VMEM_LIMIT),
        cost_estimate=cost(1 + 2.2 * heads * len(jobs) if time is None else time),
        name=name,
    )(*arrays)


def add(own, arrived):
    return (own + arrived.astype(F32)).astype(BF16)


def send(name, array, ways, axis="ctx"):
    with jax.named_scope(name):
        return lax.ppermute(array, axis, ways)


class Order:
    def __init__(self):
        self.last = None

    def gate(self, array, *others):
        held = [other for other in (self.last, *others) if other is not None]
        return lax.optimization_barrier((array, *held))[0] if held else array

    def keep(self, result):
        self.last = result[0] if isinstance(result, (list, tuple)) else result
        return result


def body(queries, key_vectors, value_vectors, attn_output, output_grad, w_out, log_total):
    rows, head_count, width = queries.shape
    ctx_count = lax.axis_size("ctx")
    head_size = lax.axis_size("head")
    head_index = lax.axis_index("head")
    ctx_index = lax.axis_index("ctx")
    group = math.gcd(ctx_count, head_count)
    group = group & -group
    heads = head_count // group
    blocks = ctx_count // group
    member = ctx_index % group
    packed_rows = rows + stat_rows(rows)
    outer = heads // 3
    inner = heads - 2 * outer
    kinds = [(0, outer), (outer, inner), (heads - outer, outer)]
    others = range(1, group)
    query_kinds = [(0, outer), (outer, heads - outer)] if outer else [(0, heads)]
    order = Order()

    def swap(d):
        return [(i, (i // group) * group + (i % group ^ d)) for i in range(ctx_count)]

    def exchange(name, pieces):
        return [send(name, piece, swap(d)) for d, piece in zip(others, pieces)]

    def shift(first, last, by):
        return [(z * group + i, (z + by) * group + i) for z in range(first, last) for i in range(group)]

    def up(step):
        return shift(step - 1, blocks - 1, 1)

    def down(step):
        return shift(1, blocks - step + 1, -1)

    def head_major(array):
        return jnp.transpose(array, (1, 0, 2))

    def head_of(d, head):
        return lambda member: ((member ^ d) * heads + head,)

    meta = [jnp.asarray(member ^ d, jnp.int32) for d in range(group)]
    if head_size == 2:
        features = [output_grad, send("features", output_grad, [(0, 1), (1, 0)], "head")]
        places = [head_index, 1 - head_index]
    else:
        features = [lax.all_gather(output_grad, "head", axis=1, tiled=True)]
        places = [jnp.zeros_like(head_index)]

    own = [head_major(queries), head_major(key_vectors), head_major(value_vectors)]
    all_heads = range(heads)
    first_in = [(i, h) for h in range(outer) for i in (1, 2)] + [(0, h) for h in range(outer, heads)]
    second_in = [(i, h) for h in range(outer, heads) for i in (1, 2)] + [(0, h) for h in range(outer)]

    wants = [first_in, second_in]
    pieces = order.keep(
        move(
            "split",
            group,
            own,
            [(len(wanted), rows, width) for wanted in wants for _ in range(group)],
            [
                (i, head_of(d, h), 3 + w * group + d, at(n))
                for w, wanted in enumerate(wants)
                for d in range(group)
                for n, (i, h) in enumerate(wanted)
            ],
            source=pltpu.HBM,
            limit=SPLIT_LIMIT,
        )
    )

    pieces = list(pieces)

    def join(name, wanted, got, arrays):
        copies = [
            (d, at(wanted.index(key)), group + target, at(d, *index))
            for target, (_, where) in enumerate(arrays)
            for key, index in where.items()
            for d in range(group)
        ]
        got = [order.gate(got[0])] + got[1:]
        return order.keep(move(name, group, got, [(group,) + shape for shape, _ in arrays], copies))

    def pair_array(first, count):
        where = {(i, first + h): (h, i - 1) for h in range(count) for i in (1, 2)}
        return (count, 2, rows, width), where

    def query_array(first, count):
        return (count, rows, width), {(0, first + h): (h,) for h in range(count)}

    got_first = pieces[:1] + exchange("first", pieces[1:group])
    flat_totals = jnp.transpose(log_total, (1, 0))
    partial = None
    for feature, place in zip(features[:-1], places):
        partial = order.keep(
            project(jnp.stack(meta + [place]), order.gate(feature), w_out, partial, head_major(attn_output), flat_totals, group, False)
        )

    up_a, down_q, down_c = [None], [None], [None]
    if outer:
        pairs_a, query_bc = join(
            "join_first", first_in, got_first, [pair_array(0, outer), query_array(outer, heads - outer)]
        )
        up_a = [pairs_a]
        if blocks > 1:
            up_a.append(send("pairs_a", pairs_a, up(1)))
    else:
        (query_bc,) = join("join_first", first_in, got_first, [query_array(0, heads)])
    down_q = [query_bc]
    if blocks > 1:
        down_q.append(send("queries", query_bc, down(1)))
    got_second = [send("second", order.gate(p), swap(d)) for d, p in zip(others, pieces[group + 1 :]) if d > 1]

    def hop(arrays, step):
        return arrays[min(step, len(arrays) - 1)]

    feature = order.gate(features[-1])
    packed = order.keep(
        project(jnp.stack(meta + [places[-1]]), feature, w_out, partial, head_major(attn_output), flat_totals, group, True)
    )
    got_grads = exchange(
        "grads",
        order.keep(
            move(
                "split_grads", group, [packed], [packed.shape[1:]] * (group - 1),
                [(0, at(d), d, at(slice(None))) for d in others],
            )
        ) if group > 1 else [],
    )
    for step in range(2, blocks):
        if outer:
            up_a.append(send("pairs_a", order.gate(up_a[-1]), up(step)))
        down_q.append(send("queries", order.gate(down_q[-1]), down(step)))
    got_second = [send("second", order.gate(p), swap(1)) for p in pieces[group + 1 : group + 2]] + got_second
    got_second = pieces[group : group + 1] + got_second
    if outer:
        pairs_b, pairs_c, query_a = join(
            "join_second",
            second_in,
            got_second,
            [pair_array(outer, inner), pair_array(heads - outer, outer), query_array(0, outer)],
        )
    else:
        (pairs_b,) = join("join_second", second_in, got_second, [pair_array(0, heads)])
    grads = order.keep(
        move(
            "join_grads",
            group,
            [order.gate(packed)] + got_grads,
            [(group, count, packed_rows, width) for _, count in query_kinds],
            [
                copy
                for target, (first, count) in enumerate(query_kinds)
                for copy in [(0, at(0, pl.ds(first, count)), group + target, at(0))]
                + [(d, at(pl.ds(first, count)), group + target, at(d)) for d in others]
            ],
        )
    )
    grad_a, grad_bc = grads if outer else (None, grads[0])

    def run(name, queries, pairs, jobs, side, count, running=None, total=F32, parts=(), wait=(), time=None):
        query, grad, f, g = queries[0]
        queries = [(order.gate(query, *wait), grad, f, g)] + list(queries[1:])
        return order.keep(
            attend(queries, pairs, jobs, side, count, group, blocks, running=running, total_type=total, part_types=parts, name=name, time=time)
        )

    far = blocks - 1
    near = range(1, far)
    final = BF16 if far == 0 else F32
    down_g = [grad_bc]
    if far:
        down_g.append(send("grads", grad_bc, down(1)))

    def leave(dq, dp):
        n_q, n_p = dq.shape[1], dp.shape[1]
        if group == 1:
            return []
        return exchange(
            "leave",
            order.keep(
                move(
                    "leave",
                    group,
                    [order.gate(dq), dp],
                    [(n_q + 2 * n_p, rows, width)] * (group - 1),
                    [(0, at(d), 1 + d, at(pl.ds(0, n_q))) for d in others]
                    + [(1, at(d, h), 1 + d, at(pl.ds(n_q + 2 * h, 2))) for d in others for h in range(n_p)],
                )
            ),
        )

    def homeward_a(step, back):
        total = order.keep(add(order.gate(parts_a[step]), back))
        return send("home_a", total, shift(step, blocks, -1)) if step else total

    def homeward_c(step, back):
        total = order.keep(add(order.gate(parts_c[step]), back))
        return send("home_c", total, shift(0, blocks - step, 1)) if step else total

    if outer:
        dp_c, dq_c = run(
            "own_c", [(query_bc, grad_bc, inner, inner)], [(pairs_c, 0)], [(0, 0, 0)], "key", outer,
            total=final, parts=[F32], wait=[hop(up_a, 2), hop(down_q, 2)],
        )
        parts_c, dq_a, back_a, back_c = [dq_c], None, None, None
    up_b = [order.gate(pairs_b)]
    if far:
        up_b.append(send("pairs_b", up_b[0], up(1)))
        if far > 1:
            down_g.append(send("grads", down_g[1], down(2)))
    if outer and far:
        dq_a, back_a = run(
            "far_a", [(query_a, grad_a, 0, 0)], [(up_a[far], 0)], [(0, 0, -far)], "query", outer,
            parts=[BF16], wait=[down_g[1]],
        )
        back_a = send("home_a", back_a, shift(far, blocks, -1))
    if outer:
        dq_a, *parts_a = run(
            "near_a", [(query_a, grad_a, 0, 0)], [(pair, 0) for pair in up_a[: max(far, 1)]],
            [(0, s, -s) for s in range(max(far, 1))], "query", outer, running=dq_a, total=BF16,
            parts=[F32] * max(far, 1), wait=[hop(down_q, far)],
        )
        dp_a = parts_a[0]
    for step in range(len(down_g), blocks):
        down_g.append(send("grads", order.gate(down_g[-1]), down(step)))
    for step in range(len(up_b), blocks):
        up_b.append(send("pairs_b", order.gate(up_b[-1]), up(step)))
    if outer and near:
        dp_c, *more = run(
            "near_c", [(down_q[s], down_g[s], inner, inner) for s in near], [(pairs_c, 0)],
            [(s - 1, 0, s) for s in near], "key", outer, running=dp_c, parts=[F32] * len(near),
            wait=[hop(up_b, 1)], time=0.1,
        )
        parts_c += more
        back_a = homeward_a(far - 1, back_a)
    if outer and far:
        dp_c, back_c = run(
            "far_c", [(down_q[far], down_g[far], inner, inner)], [(pairs_c, 0)], [(0, 0, far)], "key", outer,
            running=dp_c, total=BF16, parts=[BF16],
        )
        back_c = send("home_c", back_c, shift(0, blocks - far, 1))
    batches = []
    if outer:
        batches.append((dq_a, dp_c, 0, 2, leave(dq_a, dp_c)))
    dq_b, dp_b = run(
        "near_up_b", [(query_bc, grad_bc, 0, 0)], [(pair, 0) for pair in up_b[: max(far, 1)]],
        [(0, s, -s) for s in range(max(far, 1))], "query", inner, total=final,
        parts=[F32] + [None] * (max(far, 1) - 1),
    )
    if outer and near:
        back_c = homeward_c(far - 1, back_c)
        for step in reversed(range(1, far - 1)):
            back_a = homeward_a(step, back_a)
    if far:
        (dp_b,) = run(
            "down_b", [(down_q[s], down_g[s], 0, 0) for s in range(1, blocks)], [(pairs_b, 0)],
            [(s - 1, 0, s) for s in range(1, blocks)], "key", inner, running=dp_b, total=BF16,
            parts=[None] * far, wait=batches[0][4] if outer else [],
        )
    if outer and near:
        for step in reversed(range(1, far - 1)):
            back_c = homeward_c(step, back_c)
    if far:
        (dq_b,) = run(
            "far_up_b", [(query_bc, grad_bc, 0, 0)], [(up_b[far], 0)], [(0, 0, -far)], "query", inner,
            running=dq_b, total=BF16, parts=[None],
        )
    dp_b = dp_b.astype(BF16)
    batches.append((dq_b, dp_b, 1, 1, leave(dq_b, dp_b)))
    if outer:
        if far:
            dp_a, dq_c = homeward_a(0, back_a), homeward_c(0, back_c)
        dq_c, dp_a = dq_c.astype(BF16), dp_a.astype(BF16)
        batches.append((dq_c, dp_a, 2, 0, leave(dq_c, dp_a)))

    arrays, copies = [], []
    for dq, dp, query_kind, pair_kind, got in batches:
        base = len(arrays)
        arrays += [dq, dp] + got
        first_q, n_q = kinds[query_kind]
        first_p, n_p = kinds[pair_kind]
        for d in range(group):
            for h in range(n_q):
                source = (base, at(0, h)) if d == 0 else (base + 1 + d, at(h))
                copies.append((*source, 0, head_of(d, first_q + h)))
            for h in range(n_p):
                for i in range(2):
                    source = (base + 1, at(0, h, i)) if d == 0 else (base + 1 + d, at(n_q + 2 * h + i))
                    copies.append((*source, 1 + i, head_of(d, first_p + h)))
    count = len(arrays)
    copies = [(s, s_at, count + t, t_at) for s, s_at, t, t_at in copies]
    grads = move(
        "arrive", group, arrays, [(head_count, rows, width)] * 3, copies, source=pltpu.VMEM, target=pl.ANY
    )
    return tuple(jnp.transpose(grad, (1, 0, 2)) for grad in grads)


def solution(mesh):
    in_specs = (
        P("ctx", "head", None),
        P("ctx", "head", None),
        P("ctx", "head", None),
        P("ctx", "head", None),
        P("ctx", "head"),
        P("head", None),
        P("ctx", "head"),
    )
    out_specs = (P("ctx", "head", None), P("ctx", "head", None), P("ctx", "head", None))
    return jax.shard_map(body, mesh=mesh, in_specs=in_specs, out_specs=out_specs, check_vma=False)
```

```python
import functools
import math

import jax
import jax.numpy as jnp
from jax import lax
from jax.experimental import pallas as pl
from jax.experimental.pallas import tpu as pltpu
from jax.sharding import PartitionSpec as P

F32 = jnp.float32
BF16 = jnp.bfloat16
LANES = 128
NT = (((1,), (1,)), ((), ()))
NN = (((1,), (0,)), ((), ()))
VMEM_LIMIT = 48 * 1024 * 1024
SPLIT_LIMIT = 62 * 1024 * 1024
COST_SCALE = 1.0


def cost(microseconds):
    return pl.CostEstimate(
        flops=int(1.15e9 * COST_SCALE * microseconds),
        bytes_accessed=int(3.0e6 * COST_SCALE * microseconds),
        transcendentals=0,
    )


def dot(a, b, dims):
    return lax.dot_general(a, b, dims, preferred_element_type=F32)


def stat_rows(rows):
    return -(-6 * (rows // LANES) // 16) * 16


def write_stats(total, delta):
    rows = total.shape[1]
    halves = rows // LANES
    pieces = []
    rest = [total, delta]
    for _ in range(3):
        high = [part.astype(BF16).astype(F32) for part in rest]
        rest = [part - top for part, top in zip(rest, high)]
        for top in high:
            pieces += [top[:, i * LANES : (i + 1) * LANES] for i in range(halves)]
    spare = stat_rows(rows) - len(pieces)
    if spare:
        pieces.append(jnp.zeros((spare, LANES), F32))
    return jnp.concatenate(pieces, axis=0).astype(BF16)


def read_stats(block, rows):
    halves = rows // LANES
    values = block.astype(F32)
    span = 2 * halves
    whole = values[0:span] + values[span : 2 * span] + values[2 * span : 3 * span]
    total = jnp.concatenate([whole[i : i + 1] for i in range(halves)], axis=1)
    delta = jnp.concatenate([whole[halves + i : halves + i + 1] for i in range(halves)], axis=1)
    return total, delta


def move_kernel(*refs, group, copies):
    *arrays, sems = refs
    member = lax.axis_index("ctx") % group
    started = [
        pltpu.make_async_copy(
            arrays[source].at[source_at(member)], arrays[target].at[target_at(member)], sems.at[n]
        )
        for n, (source, source_at, target, target_at) in enumerate(copies)
    ]
    for copy in started:
        copy.start()
    for copy in started:
        copy.wait()


def move(name, group, arrays, shapes, copies, source=pl.ANY, target=pltpu.VMEM, limit=VMEM_LIMIT):
    return pl.pallas_call(
        functools.partial(move_kernel, group=group, copies=copies),
        in_specs=[pl.BlockSpec(memory_space=source)] * len(arrays),
        out_specs=[pl.BlockSpec(memory_space=target)] * len(shapes),
        out_shape=[jax.ShapeDtypeStruct(shape, BF16) for shape in shapes],
        scratch_shapes=[pltpu.SemaphoreType.DMA((len(copies),))],
        compiler_params=pltpu.CompilerParams(vmem_limit_bytes=limit),
        cost_estimate=cost(1.5),
        name=name,
    )(*arrays)


def at(*index):
    return lambda member: index


def project_kernel(meta_ref, feature_ref, weight_ref, *rest, heads, final, partial):
    grad = dot(feature_ref[...], weight_ref[...], NT)
    if partial:
        grad = grad + rest[0][...]
        rest = rest[1:]
    if not final:
        rest[0][...] = grad
        return
    out_ref, total_ref, packed_ref = rest
    _, rows, width = out_ref.shape
    grad = grad.astype(BF16)
    first = meta_ref[pl.program_id(0)] * heads
    for h in range(heads):
        mine = grad[:, h * width : (h + 1) * width]
        product = mine.astype(F32) * out_ref[h].astype(F32)
        delta = jnp.sum(jnp.transpose(product), axis=0, keepdims=True)
        total = total_ref[pl.ds(first + h, 1), :]
        packed_ref[h, 0:rows, :] = mine
        packed_ref[h, rows:, :] = write_stats(total, delta)


def project(meta, feature, w_out, partial, out_heads, totals, group, final):
    all_heads, rows, width = out_heads.shape
    heads = all_heads // group
    packed = rows + stat_rows(rows)
    span = feature.shape[1]
    by_member = pl.BlockSpec((rows, heads * width), lambda d, m: (0, d))
    arrays = [feature, w_out]
    in_specs = [
        pl.BlockSpec((rows, span), lambda d, m: (0, 0)),
        pl.BlockSpec((heads * width, span), lambda d, m: (m[d], m[group])),
    ]
    if partial is not None:
        arrays.append(partial)
        in_specs.append(by_member)
    if final:
        arrays += [out_heads, totals]
        in_specs += [
            pl.BlockSpec((heads, rows, width), lambda d, m: (m[d], 0, 0)),
            pl.BlockSpec((all_heads, rows), lambda d, m: (0, 0)),
        ]
        out_spec = pl.BlockSpec((None, heads, packed, width), lambda d, m: (d, 0, 0, 0))
        out_shape = jax.ShapeDtypeStruct((group, heads, packed, width), BF16)
    else:
        out_spec, out_shape = by_member, jax.ShapeDtypeStruct((rows, all_heads * width), F32)
    return pl.pallas_call(
        functools.partial(project_kernel, heads=heads, final=final, partial=partial is not None),
        grid_spec=pltpu.PrefetchScalarGridSpec(
            num_scalar_prefetch=1, grid=(group,), in_specs=in_specs, out_specs=out_spec
        ),
        out_shape=out_shape,
        compiler_params=pltpu.CompilerParams(vmem_limit_bytes=VMEM_LIMIT),
        cost_estimate=cost(6.5),
        name="project",
    )(meta, *arrays)


def attend_kernel(*refs, group, blocks, jobs, queries, pairs, sum_in, sum_out, parts):
    refs = list(refs)
    query_refs = [refs.pop(0) for _ in range(queries)]
    grad_refs = [refs.pop(0) for _ in range(queries)]
    pair_refs = [refs.pop(0) for _ in range(pairs)]
    start_ref = refs.pop(0) if sum_in else None
    total_ref = refs.pop(0) if sum_out else None
    part_refs = [refs.pop(0) if part else None for part in parts]
    sum_ref = refs.pop(0)
    _, rows, width = query_refs[0].shape
    span = group * rows
    factor = width ** (-0.5)
    place = lax.axis_index("ctx")
    block = place // group
    member = place % group
    sum_ref[...] = start_ref[...] if sum_in else jnp.zeros(sum_ref.shape, F32)

    def compute(query_ref, grad_ref, pair_ref, part_ref, step):
        query_sum = sum_ref if sum_ref.ndim == 3 else None
        want_query = query_sum is not None or (part_ref is not None and sum_ref.ndim == 4)
        want_key = sum_ref.ndim == 4 or part_ref is not None
        keys = pair_ref[:, 0].reshape(span, width)
        values = pair_ref[:, 1].reshape(span, width)
        key_columns = jnp.transpose(keys) if want_query else None
        dk = jnp.zeros((span, width), F32)
        dv = jnp.zeros((span, width), F32)
        for g in range(group):
            query = query_ref[g]
            grad = grad_ref[g, 0:rows, :]
            total, delta = read_stats(grad_ref[g, rows:, :], rows)
            scores = dot(keys, query, NT) * factor
            if step == 0:
                index = lax.broadcasted_iota(jnp.int32, scores.shape, 0)
                key_pos = index + (member * rows)
                for i in range(1, group):
                    shift = ((member ^ i) - i) * rows
                    key_pos = jnp.where(index >= i * rows, index + shift, key_pos)
                query_pos = lax.broadcasted_iota(jnp.int32, scores.shape, 1) + (member ^ g) * rows
                scores = jnp.where(key_pos <= query_pos, scores, -jnp.inf)
            prob = jnp.exp(scores - total)
            prob_grad = dot(values, grad, NT)
            score_grad = (prob * (prob_grad - delta)).astype(BF16)
            if want_key:
                dv = dv + dot(prob.astype(BF16), grad, NN)
                dk = dk + dot(score_grad, query, NN)
            if want_query:
                dq = jnp.transpose(dot(key_columns, score_grad, NN)) * factor
                if query_sum is not None:
                    query_sum[g] += dq
                else:
                    part_ref[g] = dq.astype(part_ref.dtype)
        if want_key:
            dk = (dk * factor).reshape(group, rows, width)
            dv = dv.reshape(group, rows, width)
            if sum_ref.ndim == 4:
                sum_ref[:, 0] += dk
                sum_ref[:, 1] += dv
            else:
                part_ref[:, 0] = dk.astype(part_ref.dtype)
                part_ref[:, 1] = dv.astype(part_ref.dtype)

    for (query_at, pair_at, step), part_ref in zip(jobs, part_refs):
        run = functools.partial(
            compute, query_refs[query_at], grad_refs[query_at], pair_refs[pair_at], part_ref, step
        )
        if step == 0:
            run()
            continue
        visible = block + step < blocks if step > 0 else block >= -step
        pl.when(visible)(run)
        if part_ref is not None:

            @pl.when(jnp.logical_not(visible))
            def _(part_ref=part_ref):
                part_ref[...] = jnp.zeros(part_ref.shape, part_ref.dtype)

    if sum_out:
        total_ref[...] = sum_ref[...].astype(total_ref.dtype)


def attend(queries, pairs, jobs, side, heads, group, blocks, running=None, total_type=None, part_types=(), name="attend", time=None):
    query_arrays = [q for q, _, _, _ in queries] + [g for _, g, _, _ in queries]
    rows, width = queries[0][0].shape[2:]
    packed = queries[0][1].shape[2]

    def spec(first, *shape):
        return pl.BlockSpec((group, None) + shape, lambda h: (0, first + h) + (0,) * len(shape))

    query_shape, pair_shape = (group, heads, rows, width), (group, heads, 2, rows, width)
    sum_shape, part_shape = (query_shape, pair_shape) if side == "query" else (pair_shape, query_shape)
    in_specs = [spec(f, rows, width) for _, _, f, _ in queries]
    in_specs += [spec(f, packed, width) for _, _, _, f in queries]
    in_specs += [spec(f, 2, rows, width) for _, f in pairs]
    arrays = query_arrays + [p for p, _ in pairs]
    if running is not None:
        arrays.append(running)
        in_specs.append(spec(0, *sum_shape[2:]))
    shapes, out_specs = [], []
    if total_type is not None:
        shapes.append(jax.ShapeDtypeStruct(sum_shape, total_type))
        out_specs.append(spec(0, *sum_shape[2:]))
    for part in part_types:
        if part is not None:
            shapes.append(jax.ShapeDtypeStruct(part_shape, part))
            out_specs.append(spec(0, *part_shape[2:]))
    return pl.pallas_call(
        functools.partial(
            attend_kernel,
            group=group,
            blocks=blocks,
            jobs=jobs,
            queries=len(queries),
            pairs=len(pairs),
            sum_in=running is not None,
            sum_out=total_type is not None,
            parts=[part is not None for part in part_types],
        ),
        grid=(heads,),
        in_specs=in_specs,
        out_specs=out_specs,
        out_shape=shapes,
        scratch_shapes=[pltpu.VMEM((group,) + sum_shape[2:], F32)],
        compiler_params=pltpu.CompilerParams(vmem_limit_bytes=VMEM_LIMIT),
        cost_estimate=cost(1 + 2.2 * heads * len(jobs) if time is None else time),
        name=name,
    )(*arrays)


def add(own, arrived):
    return (own + arrived.astype(F32)).astype(BF16)


def send(name, array, ways, axis="ctx"):
    with jax.named_scope(name):
        return lax.ppermute(array, axis, ways)


class Order:
    def __init__(self):
        self.last = None

    def gate(self, array, *others):
        held = [other for other in (self.last, *others) if other is not None]
        return lax.optimization_barrier((array, *held))[0] if held else array

    def keep(self, result):
        self.last = result[0] if isinstance(result, (list, tuple)) else result
        return result


def body(queries, key_vectors, value_vectors, attn_output, output_grad, w_out, log_total):
    rows, head_count, width = queries.shape
    ctx_count = lax.axis_size("ctx")
    head_size = lax.axis_size("head")
    head_index = lax.axis_index("head")
    ctx_index = lax.axis_index("ctx")
    group = math.gcd(ctx_count, head_count)
    group = group & -group
    heads = head_count // group
    blocks = ctx_count // group
    member = ctx_index % group
    packed_rows = rows + stat_rows(rows)
    outer = heads // 3
    inner = heads - 2 * outer
    kinds = [(0, outer), (outer, inner), (heads - outer, outer)]
    others = range(1, group)
    query_kinds = [(0, outer), (outer, heads - outer)] if outer else [(0, heads)]
    order = Order()

    def swap(d):
        return [(i, (i // group) * group + (i % group ^ d)) for i in range(ctx_count)]

    def exchange(name, pieces):
        return [send(name, piece, swap(d)) for d, piece in zip(others, pieces)]

    def shift(first, last, by):
        return [(z * group + i, (z + by) * group + i) for z in range(first, last) for i in range(group)]

    def up(step):
        return shift(step - 1, blocks - 1, 1)

    def down(step):
        return shift(1, blocks - step + 1, -1)

    def head_major(array):
        return jnp.transpose(array, (1, 0, 2))

    def head_of(d, head):
        return lambda member: ((member ^ d) * heads + head,)

    meta = [jnp.asarray(member ^ d, jnp.int32) for d in range(group)]
    if head_size == 2:
        features = [output_grad, send("features", output_grad, [(0, 1), (1, 0)], "head")]
        places = [head_index, 1 - head_index]
    else:
        features = [lax.all_gather(output_grad, "head", axis=1, tiled=True)]
        places = [jnp.zeros_like(head_index)]

    own = [head_major(queries), head_major(key_vectors), head_major(value_vectors)]
    all_heads = range(heads)
    first_in = [(i, h) for h in range(outer) for i in (1, 2)] + [(0, h) for h in range(outer, heads)]
    second_in = [(i, h) for h in range(outer, heads) for i in (1, 2)] + [(0, h) for h in range(outer)]

    wants = [first_in, second_in]
    pieces = order.keep(
        move(
            "split",
            group,
            own,
            [(len(wanted), rows, width) for wanted in wants for _ in range(group)],
            [
                (i, head_of(d, h), 3 + w * group + d, at(n))
                for w, wanted in enumerate(wants)
                for d in range(group)
                for n, (i, h) in enumerate(wanted)
            ],
            source=pltpu.HBM,
            limit=SPLIT_LIMIT,
        )
    )

    pieces = list(pieces)

    def join(name, wanted, got, arrays):
        copies = [
            (d, at(wanted.index(key)), group + target, at(d, *index))
            for target, (_, where) in enumerate(arrays)
            for key, index in where.items()
            for d in range(group)
        ]
        got = [order.gate(got[0])] + got[1:]
        return order.keep(move(name, group, got, [(group,) + shape for shape, _ in arrays], copies))

    def pair_array(first, count):
        where = {(i, first + h): (h, i - 1) for h in range(count) for i in (1, 2)}
        return (count, 2, rows, width), where

    def query_array(first, count):
        return (count, rows, width), {(0, first + h): (h,) for h in range(count)}

    got_first = pieces[:1] + exchange("first", pieces[1:group])
    flat_totals = jnp.transpose(log_total, (1, 0))
    partial = None
    for feature, place in zip(features[:-1], places):
        partial = order.keep(
            project(jnp.stack(meta + [place]), order.gate(feature), w_out, partial, head_major(attn_output), flat_totals, group, False)
        )

    up_a, down_c = [None], [None]
    if outer:
        pairs_a, query_bc = join(
            "join_first", first_in, got_first, [pair_array(0, outer), query_array(outer, heads - outer)]
        )
    else:
        (query_bc,) = join("join_first", first_in, got_first, [query_array(0, heads)])
    down_q = [query_bc]
    if blocks > 1:
        down_q.append(send("queries", query_bc, down(1)))
    if outer:
        up_a = [pairs_a]
        if blocks > 1:
            up_a.append(send("pairs_a", pairs_a, up(1)))
    got_second = [send("second", order.gate(p), swap(d)) for d, p in zip(others, pieces[group + 1 :]) if d > 1]

    def hop(arrays, step):
        return arrays[min(step, len(arrays) - 1)]

    feature = order.gate(features[-1])
    packed = order.keep(
        project(jnp.stack(meta + [places[-1]]), feature, w_out, partial, head_major(attn_output), flat_totals, group, True)
    )
    got_grads = exchange(
        "grads",
        order.keep(
            move(
                "split_grads", group, [packed], [packed.shape[1:]] * (group - 1),
                [(0, at(d), d, at(slice(None))) for d in others],
            )
        ) if group > 1 else [],
    )
    for step in range(2, blocks):
        if outer:
            up_a.append(send("pairs_a", order.gate(up_a[-1]), up(step)))
        down_q.append(send("queries", order.gate(down_q[-1]), down(step)))
    got_second = [send("second", order.gate(p), swap(1)) for p in pieces[group + 1 : group + 2]] + got_second
    got_second = pieces[group : group + 1] + got_second
    if outer:
        pairs_b, pairs_c, query_a = join(
            "join_second",
            second_in,
            got_second,
            [pair_array(outer, inner), pair_array(heads - outer, outer), query_array(0, outer)],
        )
    else:
        (pairs_b,) = join("join_second", second_in, got_second, [pair_array(0, heads)])
    grads = order.keep(
        move(
            "join_grads",
            group,
            [order.gate(packed)] + got_grads,
            [(group, count, packed_rows, width) for _, count in query_kinds],
            [
                copy
                for target, (first, count) in enumerate(query_kinds)
                for copy in [(0, at(0, pl.ds(first, count)), group + target, at(0))]
                + [(d, at(pl.ds(first, count)), group + target, at(d)) for d in others]
            ],
        )
    )
    grad_a, grad_bc = grads if outer else (None, grads[0])

    def run(name, queries, pairs, jobs, side, count, running=None, total=F32, parts=(), wait=(), time=None):
        query, grad, f, g = queries[0]
        queries = [(order.gate(query, *wait), grad, f, g)] + list(queries[1:])
        return order.keep(
            attend(queries, pairs, jobs, side, count, group, blocks, running=running, total_type=total, part_types=parts, name=name, time=time)
        )

    far = blocks - 1
    near = range(1, far)
    final = BF16 if far == 0 else F32
    down_g = [grad_bc]
    if far:
        down_g.append(send("grads", grad_bc, down(1)))

    def leave(*results):
        counts = [array.shape[1] * (array.ndim - 3) for array in results]
        copies = []
        for n, array in enumerate(results):
            start = sum(counts[:n])
            for d in others:
                target = len(results) + d - 1
                if array.ndim == 4:
                    copies.append((n, at(d), target, at(pl.ds(start, counts[n]))))
                else:
                    copies += [(n, at(d, h), target, at(pl.ds(start + 2 * h, 2))) for h in range(array.shape[1])]
        if group == 1:
            return []
        arrays = [order.gate(results[0])] + list(results[1:])
        pieces = move("leave", group, arrays, [(sum(counts), rows, width)] * (group - 1), copies)
        return exchange("leave", order.keep(pieces))

    def homeward_a(step, back):
        total = order.keep(add(order.gate(parts_a[step]), back))
        return send("home_a", total, shift(step, blocks, -1)) if step else total

    def homeward_c(step, back):
        total = order.keep(add(order.gate(parts_c[step]), back))
        return send("home_c", total, shift(0, blocks - step, 1)) if step else total

    if outer:
        dp_c, dq_c = run(
            "own_c", [(query_bc, grad_bc, inner, inner)], [(pairs_c, 0)], [(0, 0, 0)], "key", outer,
            total=final, parts=[F32], wait=[hop(up_a, 2), hop(down_q, 2)],
        )
        parts_c, dq_a, back_a, back_c = [dq_c], None, None, None
    dp_b, dq_b = run(
        "own_b", [(query_bc, grad_bc, 0, 0)], [(pairs_b, 0)], [(0, 0, 0)], "key", inner, total=final, parts=[F32]
    )
    up_b = [order.gate(pairs_b)]
    if far:
        up_b.append(send("pairs_b", up_b[0], up(1)))
        if far > 1:
            down_g.append(send("grads", down_g[1], down(2)))
    if outer and far:
        dq_a, back_a = run(
            "far_a", [(query_a, grad_a, 0, 0)], [(up_a[far], 0)], [(0, 0, -far)], "query", outer,
            parts=[BF16], wait=[down_g[1]],
        )
        back_a = send("home_a", back_a, shift(far, blocks, -1))
    if outer:
        dq_a, *parts_a = run(
            "near_a", [(query_a, grad_a, 0, 0)], [(pair, 0) for pair in up_a[: max(far, 1)]],
            [(0, s, -s) for s in range(max(far, 1))], "query", outer, running=dq_a, total=BF16,
            parts=[F32] * max(far, 1), wait=[hop(down_q, far)],
        )
        dp_a = parts_a[0]
    for step in range(len(down_g), blocks):
        down_g.append(send("grads", order.gate(down_g[-1]), down(step)))
    for step in range(len(up_b), blocks):
        up_b.append(send("pairs_b", order.gate(up_b[-1]), up(step)))
    if outer and near:
        back_a = homeward_a(far - 1, back_a)
        dp_c, *more = run(
            "near_c", [(down_q[s], down_g[s], inner, inner) for s in near], [(pairs_c, 0)],
            [(s - 1, 0, s) for s in near], "key", outer, running=dp_c, parts=[F32] * len(near),
            wait=[hop(up_b, 1)], time=0.1,
        )
        parts_c += more
    if near:
        (dp_b,) = run(
            "near_down_b", [(down_q[s], down_g[s], 0, 0) for s in near], [(pairs_b, 0)],
            [(s - 1, 0, s) for s in near], "key", inner, running=dp_b, parts=[None] * len(near), time=0.1,
        )
    if outer and far:
        for step in reversed(range(1, far - 1)):
            back_a = homeward_a(step, back_a)
        dp_c, back_c = run(
            "far_c", [(down_q[far], down_g[far], inner, inner)], [(pairs_c, 0)], [(0, 0, far)], "key", outer,
            running=dp_c, total=BF16, parts=[BF16],
        )
        back_c = send("home_c", back_c, shift(0, blocks - far, 1))
    if near:
        (dq_b,) = run(
            "near_up_b", [(query_bc, grad_bc, 0, 0)], [(up_b[s], 0) for s in near],
            [(0, s - 1, -s) for s in near], "query", inner, running=dq_b, parts=[None] * len(near), time=7.6,
        )
    batches, left = [], []
    if outer:
        batches.append([(dq_a, kinds[0]), (dp_c, kinds[2])])
        left.append(leave(dq_a, dp_c))
    if outer and near:
        back_c = homeward_c(far - 1, back_c)
    if far:
        (dp_b,) = run(
            "far_down_b", [(down_q[far], down_g[far], 0, 0)], [(pairs_b, 0)], [(0, 0, far)], "key", inner,
            running=dp_b, total=BF16, parts=[None], wait=left[0] if outer else [], time=7.6,
        )
    if far:
        (dq_b,) = run(
            "far_up_b", [(query_bc, grad_bc, 0, 0)], [(up_b[far], 0)], [(0, 0, -far)], "query", inner,
            running=dq_b, total=BF16, parts=[None],
        )
    dq_b = dq_b.astype(BF16)
    dp_b = dp_b.astype(BF16)
    batches.append([(dq_b, kinds[1]), (dp_b, kinds[1])])
    if outer:
        if far:
            dp_a = homeward_a(0, back_a)
        batches[-1].append((dp_a.astype(BF16), kinds[0]))
    left.append(leave(*[array for array, _ in batches[-1]]))
    if outer:
        if near:
            for step in reversed(range(1, far - 1)):
                back_c = homeward_c(step, back_c)
        if far:
            dq_c = homeward_c(0, back_c)
        dq_c = dq_c.astype(BF16)
        batches.append([(dq_c, kinds[2])])
        left.append(leave(dq_c))

    arrays, copies = [], []
    for batch, got in zip(batches, left):
        got_at, start = len(arrays) + len(batch), 0
        for array, (first, count) in batch:
            for h in range(count):
                for i in range(array.ndim - 3):
                    pair = array.ndim == 5
                    where = 1 + i if pair else 0
                    copies.append((len(arrays), at(0, h, i) if pair else at(0, h), where, head_of(0, first + h)))
                    copies += [(got_at + d - 1, at(start), where, head_of(d, first + h)) for d in others]
                    start += 1
            arrays.append(array)
        arrays += got
    count = len(arrays)
    copies = [(s, s_at, count + t, t_at) for s, s_at, t, t_at in copies]
    grads = move(
        "arrive", group, arrays, [(head_count, rows, width)] * 3, copies, source=pltpu.VMEM, target=pl.ANY
    )
    return tuple(jnp.transpose(grad, (1, 0, 2)) for grad in grads)


def solution(mesh):
    in_specs = (
        P("ctx", "head", None),
        P("ctx", "head", None),
        P("ctx", "head", None),
        P("ctx", "head", None),
        P("ctx", "head"),
        P("head", None),
        P("ctx", "head"),
    )
    out_specs = (P("ctx", "head", None), P("ctx", "head", None), P("ctx", "head", None))
    return jax.shard_map(body, mesh=mesh, in_specs=in_specs, out_specs=out_specs, check_vma=False)
```

```python
import functools
import math

import jax
import jax.numpy as jnp
from jax import lax
from jax.experimental import pallas as pl
from jax.experimental.pallas import tpu as pltpu
from jax.sharding import PartitionSpec as P

F32 = jnp.float32
BF16 = jnp.bfloat16
LANES = 128
NT = (((1,), (1,)), ((), ()))
NN = (((1,), (0,)), ((), ()))
VMEM_LIMIT = 48 * 1024 * 1024
SPLIT_LIMIT = 62 * 1024 * 1024
COST_SCALE = 1.0


def cost(microseconds):
    return pl.CostEstimate(
        flops=int(1.15e9 * COST_SCALE * microseconds),
        bytes_accessed=int(3.0e6 * COST_SCALE * microseconds),
        transcendentals=0,
    )


def dot(a, b, dims):
    return lax.dot_general(a, b, dims, preferred_element_type=F32)


def stat_rows(rows):
    return -(-6 * (rows // LANES) // 16) * 16


def write_stats(total, delta):
    rows = total.shape[1]
    halves = rows // LANES
    pieces = []
    rest = [total, delta]
    for _ in range(3):
        high = [part.astype(BF16).astype(F32) for part in rest]
        rest = [part - top for part, top in zip(rest, high)]
        for top in high:
            pieces += [top[:, i * LANES : (i + 1) * LANES] for i in range(halves)]
    spare = stat_rows(rows) - len(pieces)
    if spare:
        pieces.append(jnp.zeros((spare, LANES), F32))
    return jnp.concatenate(pieces, axis=0).astype(BF16)


def read_stats(block, rows):
    halves = rows // LANES
    values = block.astype(F32)
    span = 2 * halves
    whole = values[0:span] + values[span : 2 * span] + values[2 * span : 3 * span]
    total = jnp.concatenate([whole[i : i + 1] for i in range(halves)], axis=1)
    delta = jnp.concatenate([whole[halves + i : halves + i + 1] for i in range(halves)], axis=1)
    return total, delta


def move_kernel(*refs, group, copies):
    *arrays, sems = refs
    member = lax.axis_index("ctx") % group
    started = [
        pltpu.make_async_copy(
            arrays[source].at[source_at(member)], arrays[target].at[target_at(member)], sems.at[n]
        )
        for n, (source, source_at, target, target_at) in enumerate(copies)
    ]
    for copy in started:
        copy.start()
    for copy in started:
        copy.wait()


def move(name, group, arrays, shapes, copies, source=pl.ANY, target=pltpu.VMEM, limit=VMEM_LIMIT):
    return pl.pallas_call(
        functools.partial(move_kernel, group=group, copies=copies),
        in_specs=[pl.BlockSpec(memory_space=source)] * len(arrays),
        out_specs=[pl.BlockSpec(memory_space=target)] * len(shapes),
        out_shape=[jax.ShapeDtypeStruct(shape, BF16) for shape in shapes],
        scratch_shapes=[pltpu.SemaphoreType.DMA((len(copies),))],
        compiler_params=pltpu.CompilerParams(vmem_limit_bytes=limit),
        cost_estimate=cost(1.5),
        name=name,
    )(*arrays)


def at(*index):
    return lambda member: index


def project_kernel(meta_ref, feature_ref, weight_ref, *rest, heads, final, partial):
    grad = dot(feature_ref[...], weight_ref[...], NT)
    if partial:
        grad = grad + rest[0][...]
        rest = rest[1:]
    if not final:
        rest[0][...] = grad
        return
    out_ref, total_ref, packed_ref = rest
    _, rows, width = out_ref.shape
    grad = grad.astype(BF16)
    first = meta_ref[pl.program_id(0)] * heads
    for h in range(heads):
        mine = grad[:, h * width : (h + 1) * width]
        product = mine.astype(F32) * out_ref[h].astype(F32)
        delta = jnp.sum(jnp.transpose(product), axis=0, keepdims=True)
        total = total_ref[pl.ds(first + h, 1), :]
        packed_ref[h, 0:rows, :] = mine
        packed_ref[h, rows:, :] = write_stats(total, delta)


def project(meta, feature, w_out, partial, out_heads, totals, group, final):
    all_heads, rows, width = out_heads.shape
    heads = all_heads // group
    packed = rows + stat_rows(rows)
    span = feature.shape[1]
    by_member = pl.BlockSpec((rows, heads * width), lambda d, m: (0, d))
    arrays = [feature, w_out]
    in_specs = [
        pl.BlockSpec((rows, span), lambda d, m: (0, 0)),
        pl.BlockSpec((heads * width, span), lambda d, m: (m[d], m[group])),
    ]
    if partial is not None:
        arrays.append(partial)
        in_specs.append(by_member)
    if final:
        arrays += [out_heads, totals]
        in_specs += [
            pl.BlockSpec((heads, rows, width), lambda d, m: (m[d], 0, 0)),
            pl.BlockSpec((all_heads, rows), lambda d, m: (0, 0)),
        ]
        out_spec = pl.BlockSpec((None, heads, packed, width), lambda d, m: (d, 0, 0, 0))
        out_shape = jax.ShapeDtypeStruct((group, heads, packed, width), BF16)
    else:
        out_spec, out_shape = by_member, jax.ShapeDtypeStruct((rows, all_heads * width), F32)
    return pl.pallas_call(
        functools.partial(project_kernel, heads=heads, final=final, partial=partial is not None),
        grid_spec=pltpu.PrefetchScalarGridSpec(
            num_scalar_prefetch=1, grid=(group,), in_specs=in_specs, out_specs=out_spec
        ),
        out_shape=out_shape,
        compiler_params=pltpu.CompilerParams(vmem_limit_bytes=VMEM_LIMIT),
        cost_estimate=cost(6.5),
        name="project",
    )(meta, *arrays)


def attend_kernel(*refs, group, blocks, jobs, queries, pairs, sum_in, sum_out, parts):
    refs = list(refs)
    query_refs = [refs.pop(0) for _ in range(queries)]
    grad_refs = [refs.pop(0) for _ in range(queries)]
    pair_refs = [refs.pop(0) for _ in range(pairs)]
    start_ref = refs.pop(0) if sum_in else None
    total_ref = refs.pop(0) if sum_out else None
    part_refs = [refs.pop(0) if part else None for part in parts]
    sum_ref = refs.pop(0)
    _, rows, width = query_refs[0].shape
    span = group * rows
    factor = width ** (-0.5)
    place = lax.axis_index("ctx")
    block = place // group
    member = place % group
    sum_ref[...] = start_ref[...] if sum_in else jnp.zeros(sum_ref.shape, F32)

    def compute(query_ref, grad_ref, pair_ref, part_ref, step):
        query_sum = sum_ref if sum_ref.ndim == 3 else None
        want_query = query_sum is not None or (part_ref is not None and sum_ref.ndim == 4)
        want_key = sum_ref.ndim == 4 or part_ref is not None
        keys = pair_ref[:, 0].reshape(span, width)
        values = pair_ref[:, 1].reshape(span, width)
        key_columns = jnp.transpose(keys) if want_query else None
        dk = jnp.zeros((span, width), F32)
        dv = jnp.zeros((span, width), F32)
        for g in range(group):
            query = query_ref[g]
            grad = grad_ref[g, 0:rows, :]
            total, delta = read_stats(grad_ref[g, rows:, :], rows)
            scores = dot(keys, query, NT) * factor
            if step == 0:
                index = lax.broadcasted_iota(jnp.int32, scores.shape, 0)
                key_pos = index + (member * rows)
                for i in range(1, group):
                    shift = ((member ^ i) - i) * rows
                    key_pos = jnp.where(index >= i * rows, index + shift, key_pos)
                query_pos = lax.broadcasted_iota(jnp.int32, scores.shape, 1) + (member ^ g) * rows
                scores = jnp.where(key_pos <= query_pos, scores, -jnp.inf)
            prob = jnp.exp(scores - total)
            prob_grad = dot(values, grad, NT)
            score_grad = (prob * (prob_grad - delta)).astype(BF16)
            if want_key:
                dv = dv + dot(prob.astype(BF16), grad, NN)
                dk = dk + dot(score_grad, query, NN)
            if want_query:
                dq = jnp.transpose(dot(key_columns, score_grad, NN)) * factor
                if query_sum is not None:
                    query_sum[g] += dq
                else:
                    part_ref[g] = dq.astype(part_ref.dtype)
        if want_key:
            dk = (dk * factor).reshape(group, rows, width)
            dv = dv.reshape(group, rows, width)
            if sum_ref.ndim == 4:
                sum_ref[:, 0] += dk
                sum_ref[:, 1] += dv
            else:
                part_ref[:, 0] = dk.astype(part_ref.dtype)
                part_ref[:, 1] = dv.astype(part_ref.dtype)

    for (query_at, pair_at, step), part_ref in zip(jobs, part_refs):
        run = functools.partial(
            compute, query_refs[query_at], grad_refs[query_at], pair_refs[pair_at], part_ref, step
        )
        if step == 0:
            run()
            continue
        visible = block + step < blocks if step > 0 else block >= -step
        pl.when(visible)(run)
        if part_ref is not None:

            @pl.when(jnp.logical_not(visible))
            def _(part_ref=part_ref):
                part_ref[...] = jnp.zeros(part_ref.shape, part_ref.dtype)

    if sum_out:
        total_ref[...] = sum_ref[...].astype(total_ref.dtype)


def attend(queries, pairs, jobs, side, heads, group, blocks, running=None, total_type=None, part_types=(), name="attend", time=None):
    query_arrays = [q for q, _, _, _ in queries] + [g for _, g, _, _ in queries]
    rows, width = queries[0][0].shape[2:]
    packed = queries[0][1].shape[2]

    def spec(first, *shape):
        return pl.BlockSpec((group, None) + shape, lambda h: (0, first + h) + (0,) * len(shape))

    query_shape, pair_shape = (group, heads, rows, width), (group, heads, 2, rows, width)
    sum_shape, part_shape = (query_shape, pair_shape) if side == "query" else (pair_shape, query_shape)
    in_specs = [spec(f, rows, width) for _, _, f, _ in queries]
    in_specs += [spec(f, packed, width) for _, _, _, f in queries]
    in_specs += [spec(f, 2, rows, width) for _, f in pairs]
    arrays = query_arrays + [p for p, _ in pairs]
    if running is not None:
        arrays.append(running)
        in_specs.append(spec(0, *sum_shape[2:]))
    shapes, out_specs = [], []
    if total_type is not None:
        shapes.append(jax.ShapeDtypeStruct(sum_shape, total_type))
        out_specs.append(spec(0, *sum_shape[2:]))
    for part in part_types:
        if part is not None:
            shapes.append(jax.ShapeDtypeStruct(part_shape, part))
            out_specs.append(spec(0, *part_shape[2:]))
    return pl.pallas_call(
        functools.partial(
            attend_kernel,
            group=group,
            blocks=blocks,
            jobs=jobs,
            queries=len(queries),
            pairs=len(pairs),
            sum_in=running is not None,
            sum_out=total_type is not None,
            parts=[part is not None for part in part_types],
        ),
        grid=(heads,),
        in_specs=in_specs,
        out_specs=out_specs,
        out_shape=shapes,
        scratch_shapes=[pltpu.VMEM((group,) + sum_shape[2:], F32)],
        compiler_params=pltpu.CompilerParams(vmem_limit_bytes=VMEM_LIMIT),
        cost_estimate=cost(1 + 2.2 * heads * len(jobs) if time is None else time),
        name=name,
    )(*arrays)


def add(own, arrived):
    return (own + arrived.astype(F32)).astype(BF16)


def send(name, array, ways, axis="ctx"):
    with jax.named_scope(name):
        return lax.ppermute(array, axis, ways)


class Order:
    def __init__(self):
        self.last = None

    def gate(self, array, *others):
        held = [other for other in (self.last, *others) if other is not None]
        return lax.optimization_barrier((array, *held))[0] if held else array

    def keep(self, result):
        self.last = result[0] if isinstance(result, (list, tuple)) else result
        return result


def body(queries, key_vectors, value_vectors, attn_output, output_grad, w_out, log_total):
    rows, head_count, width = queries.shape
    ctx_count = lax.axis_size("ctx")
    head_size = lax.axis_size("head")
    head_index = lax.axis_index("head")
    ctx_index = lax.axis_index("ctx")
    group = math.gcd(ctx_count, head_count)
    group = group & -group
    heads = head_count // group
    blocks = ctx_count // group
    member = ctx_index % group
    packed_rows = rows + stat_rows(rows)
    outer = heads // 3
    inner = heads - 2 * outer
    kinds = [(0, outer), (outer, inner), (heads - outer, outer)]
    others = range(1, group)
    query_kinds = [(0, outer), (outer, heads - outer)] if outer else [(0, heads)]
    order = Order()

    def swap(d):
        return [(i, (i // group) * group + (i % group ^ d)) for i in range(ctx_count)]

    def exchange(name, pieces):
        return [send(name, piece, swap(d)) for d, piece in zip(others, pieces)]

    def shift(first, last, by):
        return [(z * group + i, (z + by) * group + i) for z in range(first, last) for i in range(group)]

    def up(step):
        return shift(step - 1, blocks - 1, 1)

    def down(step):
        return shift(1, blocks - step + 1, -1)

    def head_major(array):
        return jnp.transpose(array, (1, 0, 2))

    def head_of(d, head):
        return lambda member: ((member ^ d) * heads + head,)

    meta = [jnp.asarray(member ^ d, jnp.int32) for d in range(group)]
    if head_size == 2:
        features = [output_grad, send("features", output_grad, [(0, 1), (1, 0)], "head")]
        places = [head_index, 1 - head_index]
    else:
        features = [lax.all_gather(output_grad, "head", axis=1, tiled=True)]
        places = [jnp.zeros_like(head_index)]

    own = [head_major(queries), head_major(key_vectors), head_major(value_vectors)]
    all_heads = range(heads)
    first_in = [(0, h) for h in range(outer, heads)]
    first_pairs = [(i, h) for h in range(outer) for i in (1, 2)]
    second_in = [(i, h) for h in range(outer, heads) for i in (1, 2)] + [(0, h) for h in range(outer)]

    wants = [first_in, second_in] + ([first_pairs] if outer else [])
    pieces = order.keep(
        move(
            "split",
            group,
            own,
            [(len(wanted), rows, width) for wanted in wants for _ in range(group)],
            [
                (i, head_of(d, h), 3 + w * group + d, at(n))
                for w, wanted in enumerate(wants)
                for d in range(group)
                for n, (i, h) in enumerate(wanted)
            ],
            source=pltpu.HBM,
            limit=SPLIT_LIMIT,
        )
    )

    pieces = list(pieces)

    def join(name, wanted, got, arrays):
        copies = [
            (d, at(wanted.index(key)), group + target, at(d, *index))
            for target, (_, where) in enumerate(arrays)
            for key, index in where.items()
            for d in range(group)
        ]
        got = [order.gate(got[0])] + got[1:]
        return order.keep(move(name, group, got, [(group,) + shape for shape, _ in arrays], copies))

    def pair_array(first, count):
        where = {(i, first + h): (h, i - 1) for h in range(count) for i in (1, 2)}
        return (count, 2, rows, width), where

    def query_array(first, count):
        return (count, rows, width), {(0, first + h): (h,) for h in range(count)}

    got_first = pieces[:1] + exchange("first", pieces[1:group])
    got_pairs = pieces[2 * group : 2 * group + 1] + exchange("first", pieces[2 * group + 1 :])
    flat_totals = jnp.transpose(log_total, (1, 0))
    partial = None
    for feature, place in zip(features[:-1], places):
        partial = order.keep(
            project(jnp.stack(meta + [place]), order.gate(feature), w_out, partial, head_major(attn_output), flat_totals, group, False)
        )

    (query_bc,) = join("join_first", first_in, got_first, [query_array(outer, heads - outer)])
    down_q = [query_bc]
    if blocks > 1:
        down_q.append(send("queries", query_bc, down(1)))
    got_second = [send("second", order.gate(p), swap(d)) for d, p in zip(others, pieces[group + 1 : 2 * group]) if d > 1]
    up_a = [None]
    if outer:
        (pairs_a,) = join("join_pairs", first_pairs, got_pairs, [pair_array(0, outer)])
        up_a = [pairs_a]
        if blocks > 1:
            up_a.append(send("pairs_a", pairs_a, up(1)))

    def hop(arrays, step):
        return arrays[min(step, len(arrays) - 1)]

    feature = order.gate(features[-1], hop(down_q, 1))
    if blocks > 2:
        down_q.append(send("queries", down_q[1], down(2)))
    packed = order.keep(
        project(jnp.stack(meta + [places[-1]]), feature, w_out, partial, head_major(attn_output), flat_totals, group, True)
    )
    got_grads = exchange(
        "grads",
        order.keep(
            move(
                "split_grads", group, [packed], [packed.shape[1:]] * (group - 1),
                [(0, at(d), d, at(slice(None))) for d in others],
            )
        ) if group > 1 else [],
    )
    for step in range(2, blocks):
        if outer:
            up_a.append(send("pairs_a", order.gate(up_a[-1]), up(step)))
    got_second = [send("second", order.gate(p), swap(1)) for p in pieces[group + 1 : 2 * group][:1]] + got_second
    got_second = pieces[group : group + 1] + got_second
    for step in range(len(down_q), blocks):
        down_q.append(send("queries", order.gate(down_q[-1]), down(step)))
    if outer:
        pairs_b, pairs_c, query_a = join(
            "join_second",
            second_in,
            got_second,
            [pair_array(outer, inner), pair_array(heads - outer, outer), query_array(0, outer)],
        )
    else:
        (pairs_b,) = join("join_second", second_in, got_second, [pair_array(0, heads)])
    grads = order.keep(
        move(
            "join_grads",
            group,
            [order.gate(packed)] + got_grads,
            [(group, count, packed_rows, width) for _, count in query_kinds],
            [
                copy
                for target, (first, count) in enumerate(query_kinds)
                for copy in [(0, at(0, pl.ds(first, count)), group + target, at(0))]
                + [(d, at(pl.ds(first, count)), group + target, at(d)) for d in others]
            ],
        )
    )
    grad_a, grad_bc = grads if outer else (None, grads[0])

    def run(name, queries, pairs, jobs, side, count, running=None, total=F32, parts=(), wait=(), time=None):
        query, grad, f, g = queries[0]
        queries = [(order.gate(query, *wait), grad, f, g)] + list(queries[1:])
        return order.keep(
            attend(queries, pairs, jobs, side, count, group, blocks, running=running, total_type=total, part_types=parts, name=name, time=time)
        )

    far = blocks - 1
    near = range(1, far)
    final = BF16 if far == 0 else F32
    down_g = [grad_bc]
    if far:
        down_g.append(send("grads", grad_bc, down(1)))

    def leave(*results):
        counts = [array.shape[1] * (array.ndim - 3) for array in results]
        copies = []
        for n, array in enumerate(results):
            start = sum(counts[:n])
            for d in others:
                target = len(results) + d - 1
                if array.ndim == 4:
                    copies.append((n, at(d), target, at(pl.ds(start, counts[n]))))
                else:
                    copies += [(n, at(d, h), target, at(pl.ds(start + 2 * h, 2))) for h in range(array.shape[1])]
        if group == 1:
            return []
        arrays = [order.gate(results[0])] + list(results[1:])
        pieces = move("leave", group, arrays, [(sum(counts), rows, width)] * (group - 1), copies)
        return exchange("leave", order.keep(pieces))

    def homeward_a(step, back):
        total = order.keep(add(order.gate(parts_a[step]), back))
        return send("home_a", total, shift(step, blocks, -1)) if step else total

    def homeward_c(step, back):
        total = order.keep(add(order.gate(parts_c[step]), back))
        return send("home_c", total, shift(0, blocks - step, 1)) if step else total

    if outer:
        dp_c, dq_c = run(
            "own_c", [(query_bc, grad_bc, inner, inner)], [(pairs_c, 0)], [(0, 0, 0)], "key", outer,
            total=final, parts=[F32], wait=[hop(up_a, 2), hop(down_q, 2)],
        )
        parts_c, dq_a, back_a, back_c = [dq_c], None, None, None
    dp_b, dq_b = run(
        "own_b", [(query_bc, grad_bc, 0, 0)], [(pairs_b, 0)], [(0, 0, 0)], "key", inner, total=final, parts=[F32]
    )
    up_b = [order.gate(pairs_b)]
    if far:
        up_b.append(send("pairs_b", up_b[0], up(1)))
        if far > 1:
            down_g.append(send("grads", down_g[1], down(2)))
    if outer and far:
        dq_a, back_a = run(
            "far_a", [(query_a, grad_a, 0, 0)], [(up_a[far], 0)], [(0, 0, -far)], "query", outer,
            parts=[BF16], wait=[down_g[1]],
        )
        back_a = send("home_a", back_a, shift(far, blocks, -1))
    if outer:
        dq_a, *parts_a = run(
            "near_a", [(query_a, grad_a, 0, 0)], [(pair, 0) for pair in up_a[: max(far, 1)]],
            [(0, s, -s) for s in range(max(far, 1))], "query", outer, running=dq_a, total=BF16,
            parts=[F32] * max(far, 1), wait=[hop(down_q, far)],
        )
        dp_a = parts_a[0]
    for step in range(len(down_g), blocks):
        down_g.append(send("grads", order.gate(down_g[-1]), down(step)))
    for step in range(len(up_b), blocks):
        up_b.append(send("pairs_b", order.gate(up_b[-1]), up(step)))
    if outer and near:
        back_a = homeward_a(far - 1, back_a)
        dp_c, *more = run(
            "near_c", [(down_q[s], down_g[s], inner, inner) for s in near], [(pairs_c, 0)],
            [(s - 1, 0, s) for s in near], "key", outer, running=dp_c, parts=[F32] * len(near),
            wait=[hop(up_b, 1)], time=0.1,
        )
        parts_c += more
    if near:
        (dp_b,) = run(
            "near_down_b", [(down_q[s], down_g[s], 0, 0) for s in near], [(pairs_b, 0)],
            [(s - 1, 0, s) for s in near], "key", inner, running=dp_b, parts=[None] * len(near), time=0.1,
        )
    if outer and far:
        for step in reversed(range(1, far - 1)):
            back_a = homeward_a(step, back_a)
        dp_c, back_c = run(
            "far_c", [(down_q[far], down_g[far], inner, inner)], [(pairs_c, 0)], [(0, 0, far)], "key", outer,
            running=dp_c, total=BF16, parts=[BF16],
        )
        back_c = send("home_c", back_c, shift(0, blocks - far, 1))
    if near:
        (dq_b,) = run(
            "near_up_b", [(query_bc, grad_bc, 0, 0)], [(up_b[s], 0) for s in near],
            [(0, s - 1, -s) for s in near], "query", inner, running=dq_b, parts=[None] * len(near), time=7.6,
        )
    batches, left = [], []
    if outer:
        batches.append([(dq_a, kinds[0]), (dp_c, kinds[2])])
        left.append(leave(dq_a, dp_c))
    if outer and near:
        back_c = homeward_c(far - 1, back_c)
    if far:
        (dp_b,) = run(
            "far_down_b", [(down_q[far], down_g[far], 0, 0)], [(pairs_b, 0)], [(0, 0, far)], "key", inner,
            running=dp_b, total=BF16, parts=[None], time=7.6,
        )
    if far:
        (dq_b,) = run(
            "far_up_b", [(query_bc, grad_bc, 0, 0)], [(up_b[far], 0)], [(0, 0, -far)], "query", inner,
            running=dq_b, total=BF16, parts=[None], wait=left[0] if outer else [],
        )
    dq_b = dq_b.astype(BF16)
    dp_b = dp_b.astype(BF16)
    batches.append([(dq_b, kinds[1]), (dp_b, kinds[1])])
    if outer:
        if far:
            dp_a = homeward_a(0, back_a)
        batches[-1].append((dp_a.astype(BF16), kinds[0]))
    left.append(leave(*[array for array, _ in batches[-1]]))
    if outer:
        if near:
            for step in reversed(range(1, far - 1)):
                back_c = homeward_c(step, back_c)
        if far:
            dq_c = homeward_c(0, back_c)
        dq_c = dq_c.astype(BF16)
        batches.append([(dq_c, kinds[2])])
        left.append(leave(dq_c))

    arrays, copies = [], []
    for batch, got in zip(batches, left):
        got_at, start = len(arrays) + len(batch), 0
        for array, (first, count) in batch:
            for h in range(count):
                for i in range(array.ndim - 3):
                    pair = array.ndim == 5
                    where = 1 + i if pair else 0
                    copies.append((len(arrays), at(0, h, i) if pair else at(0, h), where, head_of(0, first + h)))
                    copies += [(got_at + d - 1, at(start), where, head_of(d, first + h)) for d in others]
                    start += 1
            arrays.append(array)
        arrays += got
    count = len(arrays)
    copies = [(s, s_at, count + t, t_at) for s, s_at, t, t_at in copies]
    grads = move(
        "arrive", group, arrays, [(head_count, rows, width)] * 3, copies, source=pltpu.VMEM, target=pl.ANY
    )
    return tuple(jnp.transpose(grad, (1, 0, 2)) for grad in grads)


def solution(mesh):
    in_specs = (
        P("ctx", "head", None),
        P("ctx", "head", None),
        P("ctx", "head", None),
        P("ctx", "head", None),
        P("ctx", "head"),
        P("head", None),
        P("ctx", "head"),
    )
    out_specs = (P("ctx", "head", None), P("ctx", "head", None), P("ctx", "head", None))
    return jax.shard_map(body, mesh=mesh, in_specs=in_specs, out_specs=out_specs, check_vma=False)
```

```python
import functools
import math

import jax
import jax.numpy as jnp
from jax import lax
from jax.experimental import pallas as pl
from jax.experimental.pallas import tpu as pltpu
from jax.sharding import PartitionSpec as P

F32 = jnp.float32
BF16 = jnp.bfloat16
LANES = 128
NT = (((1,), (1,)), ((), ()))
NN = (((1,), (0,)), ((), ()))
VMEM_LIMIT = 48 * 1024 * 1024
SPLIT_LIMIT = 62 * 1024 * 1024
COST_SCALE = 1.0


def cost(microseconds):
    return pl.CostEstimate(
        flops=int(1.15e9 * COST_SCALE * microseconds),
        bytes_accessed=int(3.0e6 * COST_SCALE * microseconds),
        transcendentals=0,
    )


def dot(a, b, dims):
    return lax.dot_general(a, b, dims, preferred_element_type=F32)


def stat_rows(rows):
    return -(-6 * (rows // LANES) // 16) * 16


def write_stats(total, delta):
    rows = total.shape[1]
    halves = rows // LANES
    pieces = []
    rest = [total, delta]
    for _ in range(3):
        high = [part.astype(BF16).astype(F32) for part in rest]
        rest = [part - top for part, top in zip(rest, high)]
        for top in high:
            pieces += [top[:, i * LANES : (i + 1) * LANES] for i in range(halves)]
    spare = stat_rows(rows) - len(pieces)
    if spare:
        pieces.append(jnp.zeros((spare, LANES), F32))
    return jnp.concatenate(pieces, axis=0).astype(BF16)


def read_stats(block, rows):
    halves = rows // LANES
    values = block.astype(F32)
    span = 2 * halves
    whole = values[0:span] + values[span : 2 * span] + values[2 * span : 3 * span]
    total = jnp.concatenate([whole[i : i + 1] for i in range(halves)], axis=1)
    delta = jnp.concatenate([whole[halves + i : halves + i + 1] for i in range(halves)], axis=1)
    return total, delta


def move_kernel(*refs, group, copies):
    *arrays, sems = refs
    member = lax.axis_index("ctx") % group
    started = [
        pltpu.make_async_copy(
            arrays[source].at[source_at(member)], arrays[target].at[target_at(member)], sems.at[n]
        )
        for n, (source, source_at, target, target_at) in enumerate(copies)
    ]
    for copy in started:
        copy.start()
    for copy in started:
        copy.wait()


def move(name, group, arrays, shapes, copies, source=pl.ANY, target=pltpu.VMEM, limit=VMEM_LIMIT):
    return pl.pallas_call(
        functools.partial(move_kernel, group=group, copies=copies),
        in_specs=[pl.BlockSpec(memory_space=source)] * len(arrays),
        out_specs=[pl.BlockSpec(memory_space=target)] * len(shapes),
        out_shape=[jax.ShapeDtypeStruct(shape, BF16) for shape in shapes],
        scratch_shapes=[pltpu.SemaphoreType.DMA((len(copies),))],
        compiler_params=pltpu.CompilerParams(vmem_limit_bytes=limit),
        cost_estimate=cost(1.5),
        name=name,
    )(*arrays)


def at(*index):
    return lambda member: index


def project_kernel(meta_ref, feature_ref, weight_ref, *rest, heads, final, partial):
    grad = jnp.transpose(dot(weight_ref[...], feature_ref[...], NT))
    if partial:
        grad = grad + rest[0][...]
        rest = rest[1:]
    if not final:
        rest[0][...] = grad
        return
    out_ref, total_ref, packed_ref = rest
    _, rows, width = out_ref.shape
    grad = grad.astype(BF16)
    first = meta_ref[pl.program_id(0)] * heads
    for h in range(heads):
        mine = grad[:, h * width : (h + 1) * width]
        product = mine.astype(F32) * out_ref[h].astype(F32)
        delta = jnp.sum(jnp.transpose(product), axis=0, keepdims=True)
        total = total_ref[pl.ds(first + h, 1), :]
        packed_ref[h, 0:rows, :] = mine
        packed_ref[h, rows:, :] = write_stats(total, delta)


def project(meta, feature, w_out, partial, out_heads, totals, group, final):
    all_heads, rows, width = out_heads.shape
    heads = all_heads // group
    packed = rows + stat_rows(rows)
    span = feature.shape[1]
    by_member = pl.BlockSpec((rows, heads * width), lambda d, m: (0, d))
    arrays = [feature, w_out]
    in_specs = [
        pl.BlockSpec((rows, span), lambda d, m: (0, 0)),
        pl.BlockSpec((heads * width, span), lambda d, m: (m[d], m[group])),
    ]
    if partial is not None:
        arrays.append(partial)
        in_specs.append(by_member)
    if final:
        arrays += [out_heads, totals]
        in_specs += [
            pl.BlockSpec((heads, rows, width), lambda d, m: (m[d], 0, 0)),
            pl.BlockSpec((all_heads, rows), lambda d, m: (0, 0)),
        ]
        out_spec = pl.BlockSpec((None, heads, packed, width), lambda d, m: (d, 0, 0, 0))
        out_shape = jax.ShapeDtypeStruct((group, heads, packed, width), BF16)
    else:
        out_spec, out_shape = by_member, jax.ShapeDtypeStruct((rows, all_heads * width), F32)
    return pl.pallas_call(
        functools.partial(project_kernel, heads=heads, final=final, partial=partial is not None),
        grid_spec=pltpu.PrefetchScalarGridSpec(
            num_scalar_prefetch=1, grid=(group,), in_specs=in_specs, out_specs=out_spec
        ),
        out_shape=out_shape,
        compiler_params=pltpu.CompilerParams(vmem_limit_bytes=VMEM_LIMIT),
        cost_estimate=cost(6.5),
        name="project",
    )(meta, *arrays)


def attend_kernel(*refs, group, blocks, jobs, queries, pairs, sum_in, sum_out, parts):
    refs = list(refs)
    query_refs = [refs.pop(0) for _ in range(queries)]
    grad_refs = [refs.pop(0) for _ in range(queries)]
    pair_refs = [refs.pop(0) for _ in range(pairs)]
    start_ref = refs.pop(0) if sum_in else None
    total_ref = refs.pop(0) if sum_out else None
    part_refs = [refs.pop(0) if part else None for part in parts]
    sum_ref = refs.pop(0)
    _, rows, width = query_refs[0].shape
    span = group * rows
    factor = width ** (-0.5)
    place = lax.axis_index("ctx")
    block = place // group
    member = place % group
    sum_ref[...] = start_ref[...] if sum_in else jnp.zeros(sum_ref.shape, F32)

    def compute(query_ref, grad_ref, pair_ref, part_ref, step):
        query_sum = sum_ref if sum_ref.ndim == 3 else None
        want_query = query_sum is not None or (part_ref is not None and sum_ref.ndim == 4)
        want_key = sum_ref.ndim == 4 or part_ref is not None
        keys = pair_ref[:, 0].reshape(span, width)
        values = pair_ref[:, 1].reshape(span, width)
        key_columns = jnp.transpose(keys) if want_query else None
        dk = jnp.zeros((span, width), F32)
        dv = jnp.zeros((span, width), F32)
        for g in range(group):
            query = query_ref[g]
            grad = grad_ref[g, 0:rows, :]
            total, delta = read_stats(grad_ref[g, rows:, :], rows)
            scores = dot(keys, query, NT) * factor
            if step == 0:
                index = lax.broadcasted_iota(jnp.int32, scores.shape, 0)
                key_pos = index + (member * rows)
                for i in range(1, group):
                    shift = ((member ^ i) - i) * rows
                    key_pos = jnp.where(index >= i * rows, index + shift, key_pos)
                query_pos = lax.broadcasted_iota(jnp.int32, scores.shape, 1) + (member ^ g) * rows
                scores = jnp.where(key_pos <= query_pos, scores, -jnp.inf)
            prob = jnp.exp(scores - total)
            prob_grad = dot(values, grad, NT)
            score_grad = (prob * (prob_grad - delta)).astype(BF16)
            if want_key:
                dv = dv + dot(prob.astype(BF16), grad, NN)
                dk = dk + dot(score_grad, query, NN)
            if want_query:
                dq = jnp.transpose(dot(key_columns, score_grad, NN)) * factor
                if query_sum is not None:
                    query_sum[g] += dq
                else:
                    part_ref[g] = dq.astype(part_ref.dtype)
        if want_key:
            dk = (dk * factor).reshape(group, rows, width)
            dv = dv.reshape(group, rows, width)
            if sum_ref.ndim == 4:
                sum_ref[:, 0] += dk
                sum_ref[:, 1] += dv
            else:
                part_ref[:, 0] = dk.astype(part_ref.dtype)
                part_ref[:, 1] = dv.astype(part_ref.dtype)

    for (query_at, pair_at, step), part_ref in zip(jobs, part_refs):
        run = functools.partial(
            compute, query_refs[query_at], grad_refs[query_at], pair_refs[pair_at], part_ref, step
        )
        if step == 0:
            run()
            continue
        visible = block + step < blocks if step > 0 else block >= -step
        pl.when(visible)(run)
        if part_ref is not None:

            @pl.when(jnp.logical_not(visible))
            def _(part_ref=part_ref):
                part_ref[...] = jnp.zeros(part_ref.shape, part_ref.dtype)

    if sum_out:
        total_ref[...] = sum_ref[...].astype(total_ref.dtype)


def attend(queries, pairs, jobs, side, heads, group, blocks, running=None, total_type=None, part_types=(), name="attend", time=None):
    query_arrays = [q for q, _, _, _ in queries] + [g for _, g, _, _ in queries]
    rows, width = queries[0][0].shape[2:]
    packed = queries[0][1].shape[2]

    def spec(first, *shape):
        return pl.BlockSpec((group, None) + shape, lambda h: (0, first + h) + (0,) * len(shape))

    query_shape, pair_shape = (group, heads, rows, width), (group, heads, 2, rows, width)
    sum_shape, part_shape = (query_shape, pair_shape) if side == "query" else (pair_shape, query_shape)
    in_specs = [spec(f, rows, width) for _, _, f, _ in queries]
    in_specs += [spec(f, packed, width) for _, _, _, f in queries]
    in_specs += [spec(f, 2, rows, width) for _, f in pairs]
    arrays = query_arrays + [p for p, _ in pairs]
    if running is not None:
        arrays.append(running)
        in_specs.append(spec(0, *sum_shape[2:]))
    shapes, out_specs = [], []
    if total_type is not None:
        shapes.append(jax.ShapeDtypeStruct(sum_shape, total_type))
        out_specs.append(spec(0, *sum_shape[2:]))
    for part in part_types:
        if part is not None:
            shapes.append(jax.ShapeDtypeStruct(part_shape, part))
            out_specs.append(spec(0, *part_shape[2:]))
    return pl.pallas_call(
        functools.partial(
            attend_kernel,
            group=group,
            blocks=blocks,
            jobs=jobs,
            queries=len(queries),
            pairs=len(pairs),
            sum_in=running is not None,
            sum_out=total_type is not None,
            parts=[part is not None for part in part_types],
        ),
        grid=(heads,),
        in_specs=in_specs,
        out_specs=out_specs,
        out_shape=shapes,
        scratch_shapes=[pltpu.VMEM((group,) + sum_shape[2:], F32)],
        compiler_params=pltpu.CompilerParams(vmem_limit_bytes=VMEM_LIMIT),
        cost_estimate=cost(1 + 2.2 * heads * len(jobs) if time is None else time),
        name=name,
    )(*arrays)


def add(own, arrived):
    return (own + arrived.astype(F32)).astype(BF16)


def send(name, array, ways, axis="ctx"):
    with jax.named_scope(name):
        return lax.ppermute(array, axis, ways)


class Order:
    def __init__(self):
        self.last = None

    def gate(self, array, *others):
        held = [other for other in (self.last, *others) if other is not None]
        return lax.optimization_barrier((array, *held))[0] if held else array

    def keep(self, result):
        self.last = result[0] if isinstance(result, (list, tuple)) else result
        return result


def body(queries, key_vectors, value_vectors, attn_output, output_grad, w_out, log_total):
    rows, head_count, width = queries.shape
    ctx_count = lax.axis_size("ctx")
    head_size = lax.axis_size("head")
    head_index = lax.axis_index("head")
    ctx_index = lax.axis_index("ctx")
    group = math.gcd(ctx_count, head_count)
    group = group & -group
    heads = head_count // group
    blocks = ctx_count // group
    member = ctx_index % group
    packed_rows = rows + stat_rows(rows)
    outer = heads // 3
    inner = heads - 2 * outer
    kinds = [(0, outer), (outer, inner), (heads - outer, outer)]
    others = range(1, group)
    query_kinds = [(0, outer), (outer, heads - outer)] if outer else [(0, heads)]
    order = Order()

    def swap(d):
        return [(i, (i // group) * group + (i % group ^ d)) for i in range(ctx_count)]

    def exchange(name, pieces):
        return [send(name, piece, swap(d)) for d, piece in zip(others, pieces)]

    def shift(first, last, by):
        return [(z * group + i, (z + by) * group + i) for z in range(first, last) for i in range(group)]

    def up(step):
        return shift(step - 1, blocks - 1, 1)

    def down(step):
        return shift(1, blocks - step + 1, -1)

    def head_major(array):
        return jnp.transpose(array, (1, 0, 2))

    def head_of(d, head):
        return lambda member: ((member ^ d) * heads + head,)

    meta = [jnp.asarray(member ^ d, jnp.int32) for d in range(group)]
    if head_size == 2:
        features = [output_grad, send("features", output_grad, [(0, 1), (1, 0)], "head")]
        places = [head_index, 1 - head_index]
    else:
        features = [lax.all_gather(output_grad, "head", axis=1, tiled=True)]
        places = [jnp.zeros_like(head_index)]

    own = [head_major(queries), head_major(key_vectors), head_major(value_vectors)]
    all_heads = range(heads)
    first_in = [(0, h) for h in range(outer, heads)]
    first_pairs = [(i, h) for h in range(outer) for i in (1, 2)]
    second_in = [(i, h) for h in range(outer, heads) for i in (1, 2)] + [(0, h) for h in range(outer)]

    wants = [first_in, second_in] + ([first_pairs] if outer else [])
    pieces = order.keep(
        move(
            "split",
            group,
            own,
            [(len(wanted), rows, width) for wanted in wants for _ in range(group)],
            [
                (i, head_of(d, h), 3 + w * group + d, at(n))
                for w, wanted in enumerate(wants)
                for d in range(group)
                for n, (i, h) in enumerate(wanted)
            ],
            source=pltpu.HBM,
            limit=SPLIT_LIMIT,
        )
    )

    pieces = list(pieces)

    def join(name, wanted, got, arrays):
        copies = [
            (d, at(wanted.index(key)), group + target, at(d, *index))
            for target, (_, where) in enumerate(arrays)
            for key, index in where.items()
            for d in range(group)
        ]
        got = [order.gate(got[0])] + got[1:]
        return order.keep(move(name, group, got, [(group,) + shape for shape, _ in arrays], copies))

    def pair_array(first, count):
        where = {(i, first + h): (h, i - 1) for h in range(count) for i in (1, 2)}
        return (count, 2, rows, width), where

    def query_array(first, count):
        return (count, rows, width), {(0, first + h): (h,) for h in range(count)}

    got_first = pieces[:1] + exchange("first", pieces[1:group])
    got_pairs = pieces[2 * group : 2 * group + 1] + exchange("first", pieces[2 * group + 1 :])
    flat_totals = jnp.transpose(log_total, (1, 0))
    partial = None
    for feature, place in zip(features[:-1], places):
        partial = order.keep(
            project(jnp.stack(meta + [place]), order.gate(feature), w_out, partial, head_major(attn_output), flat_totals, group, False)
        )

    (query_bc,) = join("join_first", first_in, got_first, [query_array(outer, heads - outer)])
    down_q = [query_bc]
    if blocks > 1:
        down_q.append(send("queries", query_bc, down(1)))
    got_second = [send("second", order.gate(p), swap(d)) for d, p in zip(others, pieces[group + 1 : 2 * group]) if d > 1]
    up_a = [None]
    if outer:
        (pairs_a,) = join("join_pairs", first_pairs, got_pairs, [pair_array(0, outer)])
        up_a = [pairs_a]
        if blocks > 1:
            up_a.append(send("pairs_a", pairs_a, up(1)))

    def hop(arrays, step):
        return arrays[min(step, len(arrays) - 1)]

    feature = order.gate(features[-1], hop(down_q, 1))
    if blocks > 2:
        down_q.append(send("queries", down_q[1], down(2)))
    packed = order.keep(
        project(jnp.stack(meta + [places[-1]]), feature, w_out, partial, head_major(attn_output), flat_totals, group, True)
    )
    got_grads = exchange(
        "grads",
        order.keep(
            move(
                "split_grads", group, [packed], [packed.shape[1:]] * (group - 1),
                [(0, at(d), d, at(slice(None))) for d in others],
            )
        ) if group > 1 else [],
    )
    for step in range(2, blocks):
        if outer:
            up_a.append(send("pairs_a", order.gate(up_a[-1]), up(step)))
    got_second = [send("second", order.gate(p), swap(1)) for p in pieces[group + 1 : 2 * group][:1]] + got_second
    got_second = pieces[group : group + 1] + got_second
    for step in range(len(down_q), blocks):
        down_q.append(send("queries", order.gate(down_q[-1]), down(step)))
    if outer:
        pairs_b, pairs_c, query_a = join(
            "join_second",
            second_in,
            got_second,
            [pair_array(outer, inner), pair_array(heads - outer, outer), query_array(0, outer)],
        )
    else:
        (pairs_b,) = join("join_second", second_in, got_second, [pair_array(0, heads)])
    grads = order.keep(
        move(
            "join_grads",
            group,
            [order.gate(packed)] + got_grads,
            [(group, count, packed_rows, width) for _, count in query_kinds],
            [
                copy
                for target, (first, count) in enumerate(query_kinds)
                for copy in [(0, at(0, pl.ds(first, count)), group + target, at(0))]
                + [(d, at(pl.ds(first, count)), group + target, at(d)) for d in others]
            ],
        )
    )
    grad_a, grad_bc = grads if outer else (None, grads[0])

    def run(name, queries, pairs, jobs, side, count, running=None, total=F32, parts=(), wait=(), time=None):
        query, grad, f, g = queries[0]
        queries = [(order.gate(query, *wait), grad, f, g)] + list(queries[1:])
        return order.keep(
            attend(queries, pairs, jobs, side, count, group, blocks, running=running, total_type=total, part_types=parts, name=name, time=time)
        )

    far = blocks - 1
    near = range(1, far)
    final = BF16 if far == 0 else F32
    down_g = [grad_bc]
    if far:
        down_g.append(send("grads", grad_bc, down(1)))

    def leave(*results):
        counts = [array.shape[1] * (array.ndim - 3) for array in results]
        copies = []
        for n, array in enumerate(results):
            start = sum(counts[:n])
            for d in others:
                target = len(results) + d - 1
                if array.ndim == 4:
                    copies.append((n, at(d), target, at(pl.ds(start, counts[n]))))
                else:
                    copies += [(n, at(d, h), target, at(pl.ds(start + 2 * h, 2))) for h in range(array.shape[1])]
        if group == 1:
            return []
        arrays = [order.gate(results[0])] + list(results[1:])
        pieces = move("leave", group, arrays, [(sum(counts), rows, width)] * (group - 1), copies)
        return exchange("leave", order.keep(pieces))

    def homeward_a(step, back):
        total = order.keep(add(order.gate(parts_a[step]), back))
        return send("home_a", total, shift(step, blocks, -1)) if step else total

    def homeward_c(step, back):
        total = order.keep(add(order.gate(parts_c[step]), back))
        return send("home_c", total, shift(0, blocks - step, 1)) if step else total

    if outer:
        dp_c, dq_c = run(
            "own_c", [(query_bc, grad_bc, inner, inner)], [(pairs_c, 0)], [(0, 0, 0)], "key", outer,
            total=final, parts=[F32], wait=[hop(up_a, 2), hop(down_q, 2)],
        )
        parts_c, dq_a, back_a, back_c = [dq_c], None, None, None
    dp_b, dq_b = run(
        "own_b", [(query_bc, grad_bc, 0, 0)], [(pairs_b, 0)], [(0, 0, 0)], "key", inner, total=final, parts=[F32]
    )
    up_b = [order.gate(pairs_b)]
    if far:
        up_b.append(send("pairs_b", up_b[0], up(1)))
        if far > 1:
            down_g.append(send("grads", down_g[1], down(2)))
    if outer and far:
        dq_a, back_a = run(
            "far_a", [(query_a, grad_a, 0, 0)], [(up_a[far], 0)], [(0, 0, -far)], "query", outer,
            parts=[BF16], wait=[down_g[1]],
        )
        back_a = send("home_a", back_a, shift(far, blocks, -1))
    if outer:
        dq_a, *parts_a = run(
            "near_a", [(query_a, grad_a, 0, 0)], [(pair, 0) for pair in up_a[: max(far, 1)]],
            [(0, s, -s) for s in range(max(far, 1))], "query", outer, running=dq_a, total=BF16,
            parts=[F32] * max(far, 1), wait=[hop(down_q, far)],
        )
        dp_a = parts_a[0]
    for step in range(len(down_g), blocks):
        down_g.append(send("grads", order.gate(down_g[-1]), down(step)))
    for step in range(len(up_b), blocks):
        up_b.append(send("pairs_b", order.gate(up_b[-1]), up(step)))
    if outer and near:
        back_a = homeward_a(far - 1, back_a)
        dp_c, *more = run(
            "near_c", [(down_q[s], down_g[s], inner, inner) for s in near], [(pairs_c, 0)],
            [(s - 1, 0, s) for s in near], "key", outer, running=dp_c, parts=[F32] * len(near),
            wait=[hop(up_b, 1)], time=0.1,
        )
        parts_c += more
    if near:
        (dp_b,) = run(
            "near_down_b", [(down_q[s], down_g[s], 0, 0) for s in near], [(pairs_b, 0)],
            [(s - 1, 0, s) for s in near], "key", inner, running=dp_b, parts=[None] * len(near), time=0.1,
        )
    if outer and far:
        for step in reversed(range(1, far - 1)):
            back_a = homeward_a(step, back_a)
        dp_c, back_c = run(
            "far_c", [(down_q[far], down_g[far], inner, inner)], [(pairs_c, 0)], [(0, 0, far)], "key", outer,
            running=dp_c, total=BF16, parts=[BF16],
        )
        back_c = send("home_c", back_c, shift(0, blocks - far, 1))
    if near:
        (dq_b,) = run(
            "near_up_b", [(query_bc, grad_bc, 0, 0)], [(up_b[s], 0) for s in near],
            [(0, s - 1, -s) for s in near], "query", inner, running=dq_b, parts=[None] * len(near), time=7.6,
        )
    batches, left = [], []
    if outer:
        batches.append([(dq_a, kinds[0]), (dp_c, kinds[2])])
        left.append(leave(dq_a, dp_c))
    if outer and near:
        back_c = homeward_c(far - 1, back_c)
    if far:
        (dp_b,) = run(
            "far_down_b", [(down_q[far], down_g[far], 0, 0)], [(pairs_b, 0)], [(0, 0, far)], "key", inner,
            running=dp_b, total=BF16, parts=[None], time=7.6,
        )
    if far:
        (dq_b,) = run(
            "far_up_b", [(query_bc, grad_bc, 0, 0)], [(up_b[far], 0)], [(0, 0, -far)], "query", inner,
            running=dq_b, total=BF16, parts=[None], wait=left[0] if outer else [],
        )
    dq_b = dq_b.astype(BF16)
    dp_b = dp_b.astype(BF16)
    batches.append([(dq_b, kinds[1]), (dp_b, kinds[1])])
    if outer:
        if far:
            dp_a = homeward_a(0, back_a)
        batches[-1].append((dp_a.astype(BF16), kinds[0]))
    left.append(leave(*[array for array, _ in batches[-1]]))
    if outer:
        if near:
            for step in reversed(range(1, far - 1)):
                back_c = homeward_c(step, back_c)
        if far:
            dq_c = homeward_c(0, back_c)
        dq_c = dq_c.astype(BF16)
        batches.append([(dq_c, kinds[2])])
        left.append(leave(dq_c))

    arrays, copies = [], []
    for batch, got in zip(batches, left):
        got_at, start = len(arrays) + len(batch), 0
        for array, (first, count) in batch:
            for h in range(count):
                for i in range(array.ndim - 3):
                    pair = array.ndim == 5
                    where = 1 + i if pair else 0
                    copies.append((len(arrays), at(0, h, i) if pair else at(0, h), where, head_of(0, first + h)))
                    copies += [(got_at + d - 1, at(start), where, head_of(d, first + h)) for d in others]
                    start += 1
            arrays.append(array)
        arrays += got
    count = len(arrays)
    copies = [(s, s_at, count + t, t_at) for s, s_at, t, t_at in copies]
    grads = move(
        "arrive", group, arrays, [(head_count, rows, width)] * 3, copies, source=pltpu.VMEM, target=pl.ANY
    )
    return tuple(jnp.transpose(grad, (1, 0, 2)) for grad in grads)


def solution(mesh):
    in_specs = (
        P("ctx", "head", None),
        P("ctx", "head", None),
        P("ctx", "head", None),
        P("ctx", "head", None),
        P("ctx", "head"),
        P("head", None),
        P("ctx", "head"),
    )
    out_specs = (P("ctx", "head", None), P("ctx", "head", None), P("ctx", "head", None))
    return jax.shard_map(body, mesh=mesh, in_specs=in_specs, out_specs=out_specs, check_vma=False)
```
